32 devices in a mesh: dp: 4 (over x, core), seq: 8 (over z, y).
Axes of the slice: x: 2, y: 2, z: 4, core: 2. Of those that a mesh axis runs over, the one named last changes fastest.
Arguments:
- queries: bfloat16 [4, 1024, 1024], P('dp', 'seq'), may hold values from -40 to 40
- key_rows: bfloat16 [4, 1024, 1024], P('dp', 'seq'), may hold values from -9 to 9
- value_rows: bfloat16 [4, 1024, 1024], P('dp', 'seq'), may hold values from -6 to 6
- query_tangent: bfloat16 [4, 1024, 1024], P('dp', 'seq'), may hold values from -6 to 6
- key_tangent: bfloat16 [4, 1024, 1024], P('dp', 'seq'), may hold values from -6 to 6
- value_tangent: bfloat16 [4, 1024, 1024], P('dp', 'seq'), may hold values from -6 to 6
- out_weight: bfloat16 [1024, 2048], replicated, may hold values from -0.75 to 0.75
- upstream: bfloat16 [4, 1024, 2048], P('dp', 'seq'), may hold values from -6 to 6
Outputs:
- block_out: bfloat16 [4, 1024, 2048], P('dp', 'seq')
- tangent_out: bfloat16 [4, 1024, 2048], P('dp', 'seq')
- grad_weight: float32 [1024, 2048], P(('dp', 'seq'))
- grad_query: bfloat16 [4, 1024, 1024], P('dp', 'seq')
- grad_key: bfloat16 [4, 1024, 1024], P('dp', 'seq')
- grad_value: bfloat16 [4, 1024, 1024], P('dp', 'seq')
The draws below stay inside these ranges and needn't reach their ends.
All inputs are finite; a program needn't handle non-finite values.
Results may differ from the reference program's by a relative error of at most 0.035.
Values may be sent and summed in bfloat16 or wider, within the bound.
A program may use at most 192 MiB of HBM per device.

```python
import math
import jax
import jax.numpy as jnp
from jax import lax

D = 2048
HEADS = 8
HEAD_DIM = 128
SEQ = 1024
BATCH = 4


def joint_draw(key):
    shape = (BATCH, SEQ, HEADS * HEAD_DIM)
    query_key = jax.random.fold_in(key, 11)
    keyed_key = jax.random.fold_in(key, 12)
    query_draw = jax.random.truncated_normal(query_key, -6.0, 6.0, shape, jnp.float32) * math.sqrt(2.0)
    key_draw = jax.random.truncated_normal(keyed_key, -6.0, 6.0, shape, jnp.float32) * math.sqrt(2.0)
    return (query_draw, key_draw)


def draw_queries(key, part):
    return joint_draw(key)[0].astype(jnp.bfloat16)


def draw_key_rows(key, part):
    return joint_draw(key)[1].astype(jnp.bfloat16)


def levels(rng, shape, split, smallest, top_value):
    gain, own = 1.0, jax.random.fold_in(rng, 6)
    for axis_at, parts in split:
        draws = jnp.exp(jax.random.uniform(jax.random.fold_in(own, axis_at), (parts,), jnp.float32, smallest / len(split), top_value / len(split)))
        gain = gain * jnp.repeat(draws, shape[axis_at] // parts).reshape([-1 if axis == axis_at else 1 for axis in range(len(shape))])
    return gain


def gaussian(stream_key, extent, width, limit, split=(), dtype=jnp.bfloat16):
    values = width * jax.random.normal(stream_key, extent, jnp.float32)
    if split:
        values = values * levels(stream_key, extent, split, -0.22, 0.18)
    return jnp.clip(values, -limit, limit).astype(dtype)


def setup_inputs(seed: int = 0) -> dict:
    arg_keys = jax.random.split(jax.random.key(seed), 9)
    return {
        "queries": draw_queries(jax.random.fold_in(arg_keys[8], 71), 0),
        "key_rows": draw_key_rows(jax.random.fold_in(arg_keys[8], 71), 0),
        "value_rows": gaussian(arg_keys[2], (BATCH, SEQ, HEADS * HEAD_DIM), 1.0, 6.0, ((0, 4), (1, 8))),
        "query_tangent": gaussian(arg_keys[3], (BATCH, SEQ, HEADS * HEAD_DIM), 1.0, 6.0, ((0, 4), (1, 8))),
        "key_tangent": gaussian(arg_keys[4], (BATCH, SEQ, HEADS * HEAD_DIM), 1.0, 6.0, ((0, 4), (1, 8))),
        "value_tangent": gaussian(arg_keys[5], (BATCH, SEQ, HEADS * HEAD_DIM), 1.0, 6.0, ((0, 4), (1, 8))),
        "out_weight": gaussian(arg_keys[6], (HEADS * HEAD_DIM, D), (HEADS * HEAD_DIM // 16) ** -0.5, 0.75),
        "upstream": gaussian(arg_keys[7], (BATCH, SEQ, D), 1.0, 6.0, ((0, 4), (1, 8))),
    }


def split_heads(matrix):
    return matrix.reshape(matrix.shape[0], HEADS, HEAD_DIM).transpose(1, 0, 2)

def join_heads(stacked):
    return stacked.transpose(1, 0, 2).reshape(stacked.shape[1], -1)

def head_forward(operands):
    query_head, key_head, value_head, query_tan, key_tan, value_tan = operands
    softmax_scale = HEAD_DIM ** (-0.5)
    scores = jnp.dot(query_head, key_head.T, preferred_element_type=jnp.float32) * softmax_scale
    tan_scores = (jnp.dot(query_tan, key_head.T, preferred_element_type=jnp.float32) + jnp.dot(query_head, key_tan.T, preferred_element_type=jnp.float32)) * softmax_scale
    row_max = lax.optimization_barrier(jnp.max(scores, axis=1, keepdims=True))
    exp_scores = jnp.exp(scores - row_max)
    weighted = exp_scores * tan_scores
    total = lax.optimization_barrier(jnp.sum(exp_scores, axis=1))
    tan_total = lax.optimization_barrier(jnp.sum(weighted, axis=1))
    exp_low = exp_scores.astype(jnp.bfloat16)
    main_acc = jnp.dot(exp_low, value_head, preferred_element_type=jnp.float32)
    tan_acc = jnp.dot(weighted.astype(jnp.bfloat16), value_head, preferred_element_type=jnp.float32) + jnp.dot(exp_low, value_tan, preferred_element_type=jnp.float32)
    attn_wide = main_acc / total[:, None]
    tan_attn = (tan_acc - attn_wide * tan_total[:, None]) / total[:, None]
    log_total = row_max[:, 0] + jnp.log(total)
    return (attn_wide.astype(jnp.bfloat16), tan_attn.astype(jnp.bfloat16), log_total)

def head_backward(operands):
    query_head, key_head, value_head, grad_head, attn_head, log_total = operands
    softmax_scale = HEAD_DIM ** (-0.5)
    scores = jnp.dot(query_head, key_head.T, preferred_element_type=jnp.float32) * softmax_scale
    attn_prob = jnp.exp(scores - log_total[:, None])
    grad_prob = jnp.dot(grad_head, value_head.T, preferred_element_type=jnp.float32)
    row_delta = lax.optimization_barrier(jnp.sum(grad_head.astype(jnp.float32) * attn_head.astype(jnp.float32), axis=1))
    grad_scores = (attn_prob * (grad_prob - row_delta[:, None])).astype(jnp.bfloat16)
    grad_query = (softmax_scale * jnp.dot(grad_scores, key_head, preferred_element_type=jnp.float32)).astype(jnp.bfloat16)
    grad_key = (softmax_scale * jnp.dot(grad_scores.T, query_head, preferred_element_type=jnp.float32)).astype(jnp.bfloat16)
    grad_value = jnp.dot(attn_prob.astype(jnp.bfloat16).T, grad_head, preferred_element_type=jnp.float32).astype(jnp.bfloat16)
    return (grad_query, grad_key, grad_value)

def one_sample(operands, out_weight):
    queries, key_rows, value_rows, query_tangent, key_tangent, value_tangent, upstream = operands
    forward_in = tuple((split_heads(matrix) for matrix in (queries, key_rows, value_rows, query_tangent, key_tangent, value_tangent)))
    attn_heads, tan_heads, log_total = lax.map(head_forward, forward_in)
    attn = join_heads(attn_heads)
    tan_attn = join_heads(tan_heads)
    block_wide = jnp.dot(attn, out_weight, preferred_element_type=jnp.float32)
    tan_wide = jnp.dot(tan_attn, out_weight, preferred_element_type=jnp.float32)
    cotangent = (tan_wide + upstream.astype(jnp.float32)).astype(jnp.bfloat16)
    grad_attn = jnp.dot(cotangent, out_weight.T, preferred_element_type=jnp.float32).astype(jnp.bfloat16)
    weight_part = jnp.dot(attn.T, cotangent, preferred_element_type=jnp.float32)
    backward_in = (split_heads(queries), split_heads(key_rows), split_heads(value_rows), split_heads(grad_attn), attn_heads, log_total)
    grads = lax.map(head_backward, backward_in)
    return (block_wide.astype(jnp.bfloat16), tan_wide.astype(jnp.bfloat16), weight_part, join_heads(grads[0]), join_heads(grads[1]), join_heads(grads[2]))

def reference(queries, key_rows, value_rows, query_tangent, key_tangent, value_tangent, out_weight, upstream):
    outputs = lax.map(lambda operands: one_sample(operands, out_weight), (queries, key_rows, value_rows, query_tangent, key_tangent, value_tangent, upstream))
    grad_weight = lax.optimization_barrier(jnp.sum(outputs[2], axis=0)) / math.sqrt(BATCH * SEQ)
    return (outputs[0], outputs[1], grad_weight, outputs[3], outputs[4], outputs[5])
```

```python
import functools
import math

import jax
import jax.numpy as jnp
from jax import lax
from jax.experimental import pallas as pl
from jax.experimental.pallas import tpu as pltpu
from jax.sharding import PartitionSpec as P

HEADS = 8
HEAD_DIM = 128


def to_heads(matrix):
    return matrix.reshape(matrix.shape[0], HEADS, HEAD_DIM)


def per_device(
    queries, key_rows, value_rows, query_tangent, key_tangent, value_tangent, out_weight, upstream
):
    local_q = to_heads(queries[0])
    local_tq = to_heads(query_tangent[0])
    tokens = queries.shape[1]
    attn_width = queries.shape[2]
    full_len = tokens * lax.axis_size("seq")
    softmax_scale = HEAD_DIM ** (-0.5)
    head_zeros = jnp.zeros((HEADS, tokens), jnp.float32)
    acc_zeros = jnp.zeros((tokens, HEADS, HEAD_DIM), jnp.float32)
    run_max = jnp.full((HEADS, tokens), -jnp.inf, jnp.float32)
    run_sum = head_zeros
    run_tan = head_zeros
    acc_main = acc_zeros
    acc_tan = acc_zeros
    key_piece = lax.all_gather(key_rows[0], "seq", axis=0, tiled=True)
    value_piece = lax.all_gather(value_rows[0], "seq", axis=0, tiled=True)
    key_tan_piece = lax.all_gather(key_tangent[0], "seq", axis=0, tiled=True)
    value_tan_piece = lax.all_gather(value_tangent[0], "seq", axis=0, tiled=True)
    key_heads = to_heads(key_piece)
    value_heads = to_heads(value_piece)
    key_tan_heads = to_heads(key_tan_piece)
    value_tan_heads = to_heads(value_tan_piece)
    scores = (
        jnp.einsum("thd,shd->hts", local_q, key_heads, preferred_element_type=jnp.float32)
        * softmax_scale
    )
    tan_scores = (
        jnp.einsum("thd,shd->hts", local_tq, key_heads, preferred_element_type=jnp.float32)
        + jnp.einsum("thd,shd->hts", local_q, key_tan_heads, preferred_element_type=jnp.float32)
    ) * softmax_scale
    new_max = jnp.max(scores, axis=2)
    shrink = jnp.exp(run_max - new_max)
    exp_scores = jnp.exp(scores - new_max[:, :, None])
    weighted = exp_scores * tan_scores
    run_sum = run_sum * shrink + jnp.sum(exp_scores, axis=2)
    run_tan = run_tan * shrink + jnp.sum(weighted, axis=2)
    exp_low = exp_scores.astype(jnp.bfloat16)
    weighted_low = weighted.astype(jnp.bfloat16)
    shrink_rows = shrink.T[:, :, None]
    acc_main = acc_main * shrink_rows + jnp.einsum(
        "hts,shd->thd", exp_low, value_heads, preferred_element_type=jnp.float32
    )
    acc_tan = (
        acc_tan * shrink_rows
        + jnp.einsum("hts,shd->thd", weighted_low, value_heads, preferred_element_type=jnp.float32)
        + jnp.einsum("hts,shd->thd", exp_low, value_tan_heads, preferred_element_type=jnp.float32)
    )
    key_store = key_piece
    value_store = value_piece
    folded = (new_max, run_sum, run_tan, acc_main, acc_tan, key_store, value_store)
    run_max, run_sum, run_tan, acc_main, acc_tan, key_store, value_store = folded
    sum_rows = run_sum.T[:, :, None]
    attn_wide = acc_main / sum_rows
    attn = attn_wide.astype(jnp.bfloat16)
    tan_attn = ((acc_tan - attn_wide * run_tan.T[:, :, None]) / sum_rows).astype(jnp.bfloat16)
    log_total = run_max + jnp.log(run_sum)
    attn_flat = attn.reshape(tokens, attn_width)
    tan_flat = tan_attn.reshape(tokens, attn_width)
    block_wide = jnp.dot(attn_flat, out_weight, preferred_element_type=jnp.float32)
    tan_wide = jnp.dot(tan_flat, out_weight, preferred_element_type=jnp.float32)
    cotangent = (tan_wide + upstream[0].astype(jnp.float32)).astype(jnp.bfloat16)
    grad_attn = jnp.einsum(
        "te,ke->tk", cotangent, out_weight, preferred_element_type=jnp.float32
    ).astype(jnp.bfloat16)
    grad_factor = 1.0 / math.sqrt(lax.axis_size("dp") * full_len)
    grad_heads = to_heads(grad_attn)
    row_delta = jnp.einsum("thd,thd->ht", grad_heads, attn, preferred_element_type=jnp.float32)
    key_all = to_heads(key_store)
    value_all = to_heads(value_store)
    scores_all = (
        jnp.einsum("thd,shd->hts", local_q, key_all, preferred_element_type=jnp.float32)
        * softmax_scale
    )
    attn_prob = jnp.exp(scores_all - log_total[:, :, None])
    grad_prob = jnp.einsum(
        "thd,shd->hts", grad_heads, value_all, preferred_element_type=jnp.float32
    )
    grad_scores = (attn_prob * (grad_prob - row_delta[:, :, None])).astype(jnp.bfloat16)
    grad_query = (
        softmax_scale
        * jnp.einsum("hts,shd->thd", grad_scores, key_all, preferred_element_type=jnp.float32)
    ).astype(jnp.bfloat16)
    all_lse, all_delta = (
        lax.all_gather(log_total.T, "seq", axis=0, tiled=True),
        lax.all_gather(row_delta.T, "seq", axis=0, tiled=True),
    )
    own_keys = to_heads(key_rows[0])
    own_values = to_heads(value_rows[0])
    query_piece = lax.all_gather(queries[0], "seq", axis=0, tiled=True)
    grad_piece = lax.all_gather(grad_attn, "seq", axis=0, tiled=True)
    query_heads = to_heads(query_piece)
    grad_piece_heads = to_heads(grad_piece)
    scores_piece = (
        jnp.einsum("qhd,khd->hqk", query_heads, own_keys, preferred_element_type=jnp.float32)
        * softmax_scale
    )
    prob_piece = jnp.exp(scores_piece - all_lse.T[:, :, None])
    dprob = jnp.einsum(
        "qhd,khd->hqk", grad_piece_heads, own_values, preferred_element_type=jnp.float32
    )
    dscore = (prob_piece * (dprob - all_delta.T[:, :, None])).astype(jnp.bfloat16)
    key_grad_sum = softmax_scale * jnp.einsum(
        "hqk,qhd->khd", dscore, query_heads, preferred_element_type=jnp.float32
    )
    value_grad_sum = jnp.einsum(
        "hqk,qhd->khd",
        prob_piece.astype(jnp.bfloat16),
        grad_piece_heads,
        preferred_element_type=jnp.float32,
    )
    grad_key = key_grad_sum.reshape(tokens, attn_width).astype(jnp.bfloat16)
    grad_value = value_grad_sum.reshape(tokens, attn_width).astype(jnp.bfloat16)
    grad_weight = lax.psum_scatter(
        grad_factor
        * jnp.einsum("tk,te->ke", attn_flat, cotangent, preferred_element_type=jnp.float32),
        ("dp", "seq"),
        scatter_dimension=0,
        tiled=True,
    )
    return (
        block_wide.astype(jnp.bfloat16)[None],
        tan_wide.astype(jnp.bfloat16)[None],
        grad_weight,
        grad_query.reshape(tokens, attn_width)[None],
        grad_key[None],
        grad_value[None],
    )


MESH = pl.DeviceIdType.MESH
NT = (((1,), (1,)), ((), ()))
TN = (((0,), (0,)), ((), ()))


def dotf(a, b, dims=(((1,), (0,)), ((), ()))):
    return lax.dot_general(a, b, dims, preferred_element_type=jnp.float32)


def fused_kernel(
    n, ndp, q_ref, k_ref, v_ref, tq_ref, tk_ref, tv_ref, w_hbm, up_hbm,
    block_ref, tan_ref, gw_ref, gq_out, gk_out, gv_out,
    qq, kk, vv, prob, attn_own, tan_own, attn_full, tan_full, w_ref, up_ref,
    cots, attn_dp, grad_loc, grad_own, gq_acc, gq_st, gk_st, gv_st, gw_st, gw_land,
    in_send, in_recv, fw_send, fw_recv, g_send, g_recv, gr_send, gr_recv,
    gw_send, gw_recv, cot_send, cot_recv, ad_send, ad_recv, load_sem,
):
    dp, me = lax.axis_index("dp"), lax.axis_index("seq")
    tok = q_ref.shape[0]
    hd = HEAD_DIM
    full = n * tok
    rows_dp = gw_st.shape[0]
    rows_own = rows_dp // n
    scale = HEAD_DIM ** (-0.5)
    gw_scale = 1.0 / math.sqrt(ndp * full)
    dp_peers = [dp, dp + 1 - 2 * lax.rem(dp, 2), lax.rem(dp + 2, 4), 3 - dp]

    def peer(d):
        return lax.rem(me + d, n)

    def source(d):
        return lax.rem(me + n - d, n)

    def at(i, size):
        return pl.ds(pl.multiple_of(i * size, size), size)

    barrier = pltpu.get_barrier_semaphore()
    for d in range(1, n):
        pl.semaphore_signal(barrier, inc=1, device_id=(dp, peer(d)), device_id_type=MESH)
    for j in range(1, ndp):
        pl.semaphore_signal(barrier, inc=1, device_id=(dp_peers[j], me), device_id_type=MESH)

    load_w = pltpu.make_async_copy(w_hbm, w_ref, load_sem.at[0])
    load_up = pltpu.make_async_copy(up_hbm, up_ref, load_sem.at[1])

    arrivals = (
        (q_ref, qq, 1), (k_ref, kk, 0), (tq_ref, qq, 0),
        (tk_ref, kk, 1), (v_ref, vv, 0), (tv_ref, vv, 1),
    )

    def in_copy(a, to, owner, d):
        src, dst, side = arrivals[a]
        return pltpu.make_async_remote_copy(
            src_ref=src.at[:, at(to, hd)],
            dst_ref=dst.at[at(owner, tok), pl.ds(side * hd, hd)],
            send_sem=in_send.at[a, d], recv_sem=in_recv.at[a, d],
            device_id=(dp, to), device_id_type=MESH,
        )

    def in_local(a):
        src, dst, side = arrivals[a]
        return pltpu.make_async_copy(
            src.at[:, at(me, hd)], dst.at[at(me, tok), pl.ds(side * hd, hd)], in_recv.at[a, 0]
        )

    for a in range(6):
        in_local(a).start()
    pl.semaphore_wait(barrier, n - 1 + ndp - 1)
    for a in range(6):
        @pl.loop(1, n)
        def _(d):
            in_copy(a, peer(d), me, d).start()
    load_w.start()
    load_up.start()

    def in_wait(a):
        in_local(a).wait()

        @pl.loop(1, n)
        def _(d):
            in_copy(a, source(d), source(d), d).wait_recv()

    for a in range(6):
        in_wait(a)

    def fw_copy(i, to, owner, d):
        src, dst = ((attn_own, attn_full), (tan_own, tan_full))[i]
        return pltpu.make_async_remote_copy(
            src_ref=src.at[at(to, tok), :],
            dst_ref=dst.at[:, at(owner, hd)],
            send_sem=fw_send.at[i, d], recv_sem=fw_recv.at[i, d],
            device_id=(dp, to), device_id_type=MESH,
        )

    def fw_local(i):
        src, dst = ((attn_own, attn_full), (tan_own, tan_full))[i]
        return pltpu.make_async_copy(
            src.at[at(me, tok), :], dst.at[:, at(me, hd)], fw_recv.at[i, 0]
        )

    span = 2 * tok
    parts = n // 2

    @pl.loop(0, parts)
    def _(j):
        p = lax.rem(me // 2 + 1 + j, parts)
        rows = at(p, span)
        q2 = qq[rows, :]
        s = dotf(q2[:, hd:], kk[:, :hd], NT)
        e = jnp.exp((s - jnp.max(s, axis=1, keepdims=True)) * scale)
        wgt = e * dotf(q2, kk[...], NT)
        total = jnp.sum(e, axis=1, keepdims=True)
        tan_total = jnp.sum(wgt, axis=1, keepdims=True) * scale
        inv = 1.0 / total
        both = dotf(e.astype(jnp.bfloat16), vv[...])
        acc_t = dotf(wgt.astype(jnp.bfloat16), vv[:, :hd]) * scale + both[:, hd:]
        wide = both[:, :hd] * inv
        attn_own[rows, :] = wide.astype(jnp.bfloat16)
        tan_own[rows, :] = ((acc_t - wide * tan_total) * inv).astype(jnp.bfloat16)
        pb = (e * inv).astype(jnp.bfloat16)
        for c in range(parts):
            prob[c, rows, :] = pb[:, c * span:(c + 1) * span]
        for half in range(2):
            owner = 2 * p + half
            d = lax.rem(owner + n - me, n)

            @pl.when(d != 0)
            def _():
                fw_copy(1, owner, me, d).start()
                fw_copy(0, owner, me, d).start()

            @pl.when(d == 0)
            def _():
                fw_local(1).start()
                fw_local(0).start()

    load_w.wait()
    load_up.wait()

    def fw_wait(i):
        fw_local(i).wait()

        @pl.loop(1, n)
        def _(d):
            fw_copy(i, source(d), source(d), d).wait_recv()

    fw_wait(1)
    ty = dotf(tan_full[...], w_ref[...])
    tan_ref[...] = ty.astype(jnp.bfloat16)
    cot = (ty + up_ref[...].astype(jnp.float32)).astype(jnp.bfloat16)
    cots[pl.ds(0, tok), :] = cot
    grad_loc[...] = dotf(cot, w_ref[...], NT).astype(jnp.bfloat16)

    def g_copy(to, owner, d):
        return pltpu.make_async_remote_copy(
            src_ref=grad_loc.at[:, at(to, hd)],
            dst_ref=grad_own.at[at(owner, tok), :],
            send_sem=g_send.at[d], recv_sem=g_recv.at[d],
            device_id=(dp, to), device_id_type=MESH,
        )

    g_local = pltpu.make_async_copy(
        grad_loc.at[:, at(me, hd)], grad_own.at[at(me, tok), :], g_recv.at[0]
    )
    g_local.start()

    @pl.loop(1, n)
    def _(d):
        g_copy(peer(d), me, d).start()

    def cot_copy(src_slot, dst_slot, to):
        return pltpu.make_async_remote_copy(
            src_ref=cots.at[pl.ds(src_slot * tok, tok), :],
            dst_ref=cots.at[pl.ds(dst_slot * tok, tok), :],
            send_sem=cot_send.at[dst_slot], recv_sem=cot_recv.at[dst_slot],
            device_id=(to, me), device_id_type=MESH,
        )

    cot_x = cot_copy(0, 2, dp_peers[2])
    cot_core = cot_copy(0, 1, dp_peers[1])
    cot_fwd = cot_copy(2, 3, dp_peers[1])
    cot_x.start()
    cot_core.start()

    fw_wait(0)

    def ad_copy(j):
        return pltpu.make_async_remote_copy(
            src_ref=attn_full.at[:, at(dp_peers[j], rows_dp)],
            dst_ref=attn_dp.at[pl.ds(j * tok, tok), :],
            send_sem=ad_send.at[j], recv_sem=ad_recv.at[j],
            device_id=(dp_peers[j], me), device_id_type=MESH,
        )

    ad_local = pltpu.make_async_copy(
        attn_full.at[:, at(dp, rows_dp)], attn_dp.at[pl.ds(0, tok), :], ad_recv.at[0]
    )
    for j in range(1, ndp):
        ad_copy(j).start()
    ad_local.start()
    block_ref[...] = dotf(attn_full[...], w_ref[...]).astype(jnp.bfloat16)

    g_local.wait()

    @pl.loop(1, n)
    def _(d):
        g_copy(source(d), source(d), d).wait_recv()

    outs = ((gk_st, gk_out), (gv_st, gv_out), (gq_st, gq_out))

    def gr_copy(i, to, owner, d):
        src, dst = outs[i]
        return pltpu.make_async_remote_copy(
            src_ref=src.at[at(to, tok), :],
            dst_ref=dst.at[:, at(owner, hd)],
            send_sem=gr_send.at[i, d], recv_sem=gr_recv.at[i, d],
            device_id=(dp, to), device_id_type=MESH,
        )

    def gr_local(i):
        src, dst = outs[i]
        return pltpu.make_async_copy(
            src.at[at(me, tok), :], dst.at[:, at(me, hd)], gr_recv.at[i, 0]
        )

    g_all = grad_own[...]
    delta = jnp.sum(
        g_all.astype(jnp.float32) * attn_own[...].astype(jnp.float32), axis=1, keepdims=True
    )
    gq_acc[...] = jnp.zeros_like(gq_acc)

    def back_chunk(j):
        p = lax.rem(me // 2 + 1 + j, parts)
        rows = at(p, span)
        pc = prob[p]
        dprob = dotf(g_all, vv[rows, :hd], NT)
        ds = (pc.astype(jnp.float32) * (dprob - delta)).astype(jnp.bfloat16)
        gq_acc[...] += dotf(ds, kk[rows, :hd])
        gk_st[rows, :] = (dotf(qq[:, hd:], ds, TN).T * scale).astype(jnp.bfloat16)
        gv_st[rows, :] = dotf(g_all, pc, TN).T.astype(jnp.bfloat16)
        for half in range(2):
            owner = 2 * p + half
            d = lax.rem(owner + n - me, n)

            @pl.when(d != 0)
            def _():
                gr_copy(0, owner, me, d).start()
                gr_copy(1, owner, me, d).start()

            @pl.when(d == 0)
            def _():
                gr_local(0).start()
                gr_local(1).start()

    def gw_copy(to, d):
        return pltpu.make_async_remote_copy(
            src_ref=gw_st.at[at(to, rows_own), :],
            dst_ref=gw_land.at[d],
            send_sem=gw_send.at[d], recv_sem=gw_recv.at[d],
            device_id=(dp, to), device_id_type=MESH,
        )

    first = parts // 2

    @pl.loop(0, first)
    def _(j):
        back_chunk(j)

    cot_x.wait_recv()
    cot_fwd.start()
    cot_core.wait_recv()
    ad_local.wait()
    for j in range(1, ndp):
        ad_copy(j).wait_recv()
    cot_fwd.wait_recv()
    gw_st[...] = (dotf(attn_dp[...], cots[...], TN) * gw_scale).astype(jnp.bfloat16)

    @pl.loop(1, n)
    def _(d):
        gw_copy(peer(d), d).start()

    @pl.loop(first, parts)
    def _(j):
        back_chunk(j)

    gq_st[...] = (gq_acc[...] * scale).astype(jnp.bfloat16)
    gr_local(2).start()

    @pl.loop(1, n)
    def _(d):
        gr_copy(2, peer(d), me, d).start()

    gw_total = gw_st[at(me, rows_own), :].astype(jnp.float32)
    for d in range(1, n):
        gw_copy(source(d), d).wait_recv()
        gw_total = gw_total + gw_land[d].astype(jnp.float32)
    gw_ref[...] = gw_total

    for i in range(3):
        gr_local(i).wait()

        @pl.loop(1, n)
        def _(d):
            gr_copy(i, source(d), source(d), d).wait_recv()

    @pl.loop(1, n)
    def _(d):
        to = peer(d)
        for a in range(6):
            in_copy(a, to, me, d).wait_send()
        for i in range(2):
            fw_copy(i, to, me, d).wait_send()
        g_copy(to, me, d).wait_send()
        gw_copy(to, d).wait_send()
        for i in range(3):
            gr_copy(i, to, me, d).wait_send()

    cot_x.wait_send()
    cot_core.wait_send()
    cot_fwd.wait_send()
    for j in range(1, ndp):
        ad_copy(j).wait_send()


def by_heads(
    queries, key_rows, value_rows, query_tangent, key_tangent, value_tangent, out_weight, upstream
):
    n, ndp = lax.axis_size("seq"), lax.axis_size("dp")
    tok, width = queries.shape[1:]
    model = out_weight.shape[1]
    full = n * tok
    hd = HEAD_DIM
    bf, f32 = jnp.bfloat16, jnp.float32
    rows_dp = width // ndp
    rows_own = rows_dp // n
    any_spec = pl.BlockSpec(memory_space=pl.ANY)
    vmem = pl.BlockSpec(memory_space=pltpu.VMEM)
    dma = pltpu.SemaphoreType.DMA
    flops = 2 * full * full * hd * 10 + 8 * tok * width * model
    outs = pl.pallas_call(
        functools.partial(fused_kernel, n, ndp),
        out_shape=(
            jax.ShapeDtypeStruct((tok, model), bf),
            jax.ShapeDtypeStruct((tok, model), bf),
            jax.ShapeDtypeStruct((rows_own, model), f32),
            jax.ShapeDtypeStruct((tok, width), bf),
            jax.ShapeDtypeStruct((tok, width), bf),
            jax.ShapeDtypeStruct((tok, width), bf),
        ),
        in_specs=[any_spec] * 8,
        out_specs=(vmem, vmem, vmem, any_spec, any_spec, any_spec),
        scratch_shapes=[
            pltpu.VMEM((full, 2 * hd), bf),
            pltpu.VMEM((full, 2 * hd), bf),
            pltpu.VMEM((full, 2 * hd), bf),
            pltpu.VMEM((n // 2, full, 2 * tok), bf),
            pltpu.VMEM((full, hd), bf),
            pltpu.VMEM((full, hd), bf),
            pltpu.VMEM((tok, width), bf),
            pltpu.VMEM((tok, width), bf),
            pltpu.VMEM((width, model), bf),
            pltpu.VMEM((tok, model), bf),
            pltpu.VMEM((ndp * tok, model), bf),
            pltpu.VMEM((ndp * tok, rows_dp), bf),
            pltpu.VMEM((tok, width), bf),
            pltpu.VMEM((full, hd), bf),
            pltpu.VMEM((full, hd), f32),
            pltpu.VMEM((full, hd), bf),
            pltpu.VMEM((full, hd), bf),
            pltpu.VMEM((full, hd), bf),
            pltpu.VMEM((rows_dp, model), bf),
            pltpu.VMEM((n, rows_own, model), bf),
            dma((6, n)), dma((6, n)), dma((2, n)), dma((2, n)), dma((n,)), dma((n,)),
            dma((3, n)), dma((3, n)), dma((n,)), dma((n,)), dma((ndp,)), dma((ndp,)),
            dma((ndp,)), dma((ndp,)), dma((2,)),
        ],
        compiler_params=pltpu.CompilerParams(
            collective_id=0, has_side_effects=True, vmem_limit_bytes=52 * 1024 * 1024
        ),
        cost_estimate=pl.CostEstimate(
            flops=flops, bytes_accessed=20 * tok * width, transcendentals=full * full
        ),
    )(
        queries[0], key_rows[0], value_rows[0], query_tangent[0], key_tangent[0],
        value_tangent[0], out_weight, upstream[0],
    )
    block, tan, gw, gq, gk, gv = outs
    return block[None], tan[None], gw, gq[None], gk[None], gv[None]


def solution(mesh):
    fits = mesh.shape["seq"] == HEADS and mesh.shape["dp"] == 4
    placed = (
        P("dp", "seq", None),
        P("dp", "seq", None),
        P("dp", "seq", None),
        P("dp", "seq", None),
        P("dp", "seq", None),
        P("dp", "seq", None),
        P(),
        P("dp", "seq", None),
    )
    return jax.shard_map(
        by_heads if fits else per_device,
        mesh=mesh,
        in_specs=placed,
        out_specs=(
            P("dp", "seq", None),
            P("dp", "seq", None),
            P(("dp", "seq"), None),
            P("dp", "seq", None),
            P("dp", "seq", None),
            P("dp", "seq", None),
        ),
        check_vma=False,
    )
```

```python
import functools
import math

import jax
import jax.numpy as jnp
from jax import lax
from jax.experimental import pallas as pl
from jax.experimental.pallas import tpu as pltpu
from jax.sharding import PartitionSpec as P

HEADS = 8
HEAD_DIM = 128


def to_heads(matrix):
    return matrix.reshape(matrix.shape[0], HEADS, HEAD_DIM)


def per_device(
    queries, key_rows, value_rows, query_tangent, key_tangent, value_tangent, out_weight, upstream
):
    local_q = to_heads(queries[0])
    local_tq = to_heads(query_tangent[0])
    tokens = queries.shape[1]
    attn_width = queries.shape[2]
    full_len = tokens * lax.axis_size("seq")
    softmax_scale = HEAD_DIM ** (-0.5)
    head_zeros = jnp.zeros((HEADS, tokens), jnp.float32)
    acc_zeros = jnp.zeros((tokens, HEADS, HEAD_DIM), jnp.float32)
    run_max = jnp.full((HEADS, tokens), -jnp.inf, jnp.float32)
    run_sum = head_zeros
    run_tan = head_zeros
    acc_main = acc_zeros
    acc_tan = acc_zeros
    key_piece = lax.all_gather(key_rows[0], "seq", axis=0, tiled=True)
    value_piece = lax.all_gather(value_rows[0], "seq", axis=0, tiled=True)
    key_tan_piece = lax.all_gather(key_tangent[0], "seq", axis=0, tiled=True)
    value_tan_piece = lax.all_gather(value_tangent[0], "seq", axis=0, tiled=True)
    key_heads = to_heads(key_piece)
    value_heads = to_heads(value_piece)
    key_tan_heads = to_heads(key_tan_piece)
    value_tan_heads = to_heads(value_tan_piece)
    scores = (
        jnp.einsum("thd,shd->hts", local_q, key_heads, preferred_element_type=jnp.float32)
        * softmax_scale
    )
    tan_scores = (
        jnp.einsum("thd,shd->hts", local_tq, key_heads, preferred_element_type=jnp.float32)
        + jnp.einsum("thd,shd->hts", local_q, key_tan_heads, preferred_element_type=jnp.float32)
    ) * softmax_scale
    new_max = jnp.max(scores, axis=2)
    shrink = jnp.exp(run_max - new_max)
    exp_scores = jnp.exp(scores - new_max[:, :, None])
    weighted = exp_scores * tan_scores
    run_sum = run_sum * shrink + jnp.sum(exp_scores, axis=2)
    run_tan = run_tan * shrink + jnp.sum(weighted, axis=2)
    exp_low = exp_scores.astype(jnp.bfloat16)
    weighted_low = weighted.astype(jnp.bfloat16)
    shrink_rows = shrink.T[:, :, None]
    acc_main = acc_main * shrink_rows + jnp.einsum(
        "hts,shd->thd", exp_low, value_heads, preferred_element_type=jnp.float32
    )
    acc_tan = (
        acc_tan * shrink_rows
        + jnp.einsum("hts,shd->thd", weighted_low, value_heads, preferred_element_type=jnp.float32)
        + jnp.einsum("hts,shd->thd", exp_low, value_tan_heads, preferred_element_type=jnp.float32)
    )
    key_store = key_piece
    value_store = value_piece
    folded = (new_max, run_sum, run_tan, acc_main, acc_tan, key_store, value_store)
    run_max, run_sum, run_tan, acc_main, acc_tan, key_store, value_store = folded
    sum_rows = run_sum.T[:, :, None]
    attn_wide = acc_main / sum_rows
    attn = attn_wide.astype(jnp.bfloat16)
    tan_attn = ((acc_tan - attn_wide * run_tan.T[:, :, None]) / sum_rows).astype(jnp.bfloat16)
    log_total = run_max + jnp.log(run_sum)
    attn_flat = attn.reshape(tokens, attn_width)
    tan_flat = tan_attn.reshape(tokens, attn_width)
    block_wide = jnp.dot(attn_flat, out_weight, preferred_element_type=jnp.float32)
    tan_wide = jnp.dot(tan_flat, out_weight, preferred_element_type=jnp.float32)
    cotangent = (tan_wide + upstream[0].astype(jnp.float32)).astype(jnp.bfloat16)
    grad_attn = jnp.einsum(
        "te,ke->tk", cotangent, out_weight, preferred_element_type=jnp.float32
    ).astype(jnp.bfloat16)
    grad_factor = 1.0 / math.sqrt(lax.axis_size("dp") * full_len)
    grad_heads = to_heads(grad_attn)
    row_delta = jnp.einsum("thd,thd->ht", grad_heads, attn, preferred_element_type=jnp.float32)
    key_all = to_heads(key_store)
    value_all = to_heads(value_store)
    scores_all = (
        jnp.einsum("thd,shd->hts", local_q, key_all, preferred_element_type=jnp.float32)
        * softmax_scale
    )
    attn_prob = jnp.exp(scores_all - log_total[:, :, None])
    grad_prob = jnp.einsum(
        "thd,shd->hts", grad_heads, value_all, preferred_element_type=jnp.float32
    )
    grad_scores = (attn_prob * (grad_prob - row_delta[:, :, None])).astype(jnp.bfloat16)
    grad_query = (
        softmax_scale
        * jnp.einsum("hts,shd->thd", grad_scores, key_all, preferred_element_type=jnp.float32)
    ).astype(jnp.bfloat16)
    all_lse, all_delta = (
        lax.all_gather(log_total.T, "seq", axis=0, tiled=True),
        lax.all_gather(row_delta.T, "seq", axis=0, tiled=True),
    )
    own_keys = to_heads(key_rows[0])
    own_values = to_heads(value_rows[0])
    query_piece = lax.all_gather(queries[0], "seq", axis=0, tiled=True)
    grad_piece = lax.all_gather(grad_attn, "seq", axis=0, tiled=True)
    query_heads = to_heads(query_piece)
    grad_piece_heads = to_heads(grad_piece)
    scores_piece = (
        jnp.einsum("qhd,khd->hqk", query_heads, own_keys, preferred_element_type=jnp.float32)
        * softmax_scale
    )
    prob_piece = jnp.exp(scores_piece - all_lse.T[:, :, None])
    dprob = jnp.einsum(
        "qhd,khd->hqk", grad_piece_heads, own_values, preferred_element_type=jnp.float32
    )
    dscore = (prob_piece * (dprob - all_delta.T[:, :, None])).astype(jnp.bfloat16)
    key_grad_sum = softmax_scale * jnp.einsum(
        "hqk,qhd->khd", dscore, query_heads, preferred_element_type=jnp.float32
    )
    value_grad_sum = jnp.einsum(
        "hqk,qhd->khd",
        prob_piece.astype(jnp.bfloat16),
        grad_piece_heads,
        preferred_element_type=jnp.float32,
    )
    grad_key = key_grad_sum.reshape(tokens, attn_width).astype(jnp.bfloat16)
    grad_value = value_grad_sum.reshape(tokens, attn_width).astype(jnp.bfloat16)
    grad_weight = lax.psum_scatter(
        grad_factor
        * jnp.einsum("tk,te->ke", attn_flat, cotangent, preferred_element_type=jnp.float32),
        ("dp", "seq"),
        scatter_dimension=0,
        tiled=True,
    )
    return (
        block_wide.astype(jnp.bfloat16)[None],
        tan_wide.astype(jnp.bfloat16)[None],
        grad_weight,
        grad_query.reshape(tokens, attn_width)[None],
        grad_key[None],
        grad_value[None],
    )


MESH = pl.DeviceIdType.MESH
NT = (((1,), (1,)), ((), ()))
TN = (((0,), (0,)), ((), ()))


def dotf(a, b, dims=(((1,), (0,)), ((), ()))):
    return lax.dot_general(a, b, dims, preferred_element_type=jnp.float32)


def fused_kernel(
    n, ndp, q_ref, k_ref, v_ref, tq_ref, tk_ref, tv_ref, w_hbm, up_hbm,
    block_hbm, tan_hbm, gw_hbm, gq_out, gk_out, gv_out,
    qq, kk, vv, prob, attn_own, tan_own, attn_full, tan_full, w_ref, up_ref,
    cots, attn_dp, grad_loc, grad_own, gq_acc, gq_st, gk_st, gv_st, gw_st, gw_land,
    e_ref, e_low, w_low, block_ref, tan_ref, gw_ref, cross_st, cross_land,
    inv_ref, ut_ref, acc_ref,
    in_send, in_recv, fw_send, fw_recv, g_send, g_recv, gr_send, gr_recv,
    gw_send, gw_recv, cot_send, cot_recv, ad_send, ad_recv, load_sem, cross_send, cross_recv, out_sem,
):
    dp, me = lax.axis_index("dp"), lax.axis_index("seq")
    tok = q_ref.shape[0]
    hd = HEAD_DIM
    full = n * tok
    rows_own = gw_st.shape[2]
    rows_dp = n * rows_own
    scale = HEAD_DIM ** (-0.5)
    gw_scale = 1.0 / math.sqrt(ndp * full)
    dp_peers = [dp, dp + 1 - 2 * lax.rem(dp, 2), lax.rem(dp + 2, 4), 3 - dp]

    def peer(d):
        return lax.rem(me + d, n)

    def source(d):
        return lax.rem(me + n - d, n)

    def far_first(i):
        return n // 2 + (1 - 2 * lax.rem(i, 2)) * ((i + 1) // 2)

    def at(i, size):
        return pl.ds(pl.multiple_of(i * size, size), size)

    barrier = pltpu.get_barrier_semaphore()
    for d in range(1, n):
        pl.semaphore_signal(barrier, inc=1, device_id=(dp, peer(d)), device_id_type=MESH)
    for j in range(1, ndp):
        pl.semaphore_signal(barrier, inc=1, device_id=(dp_peers[j], me), device_id_type=MESH)

    load_w = pltpu.make_async_copy(w_hbm, w_ref, load_sem.at[0])
    load_up = pltpu.make_async_copy(up_hbm, up_ref, load_sem.at[1])

    arrivals = (
        (q_ref, qq, 1), (k_ref, kk, 0), (tq_ref, qq, 0),
        (tk_ref, kk, 1), (v_ref, vv, 0), (tv_ref, vv, 1),
    )

    def in_copy(a, to, owner, d):
        src, dst, side = arrivals[a]
        return pltpu.make_async_remote_copy(
            src_ref=src.at[:, at(to, hd)],
            dst_ref=dst.at[at(owner, tok), pl.ds(side * hd, hd)],
            send_sem=in_send.at[a, d], recv_sem=in_recv.at[a, d],
            device_id=(dp, to), device_id_type=MESH,
        )

    def in_local(a):
        src, dst, side = arrivals[a]
        return pltpu.make_async_copy(
            src.at[:, at(me, hd)], dst.at[at(me, tok), pl.ds(side * hd, hd)], in_recv.at[a, 0]
        )

    for a in range(6):
        in_local(a).start()
    pl.semaphore_wait(barrier, n - 1 + ndp - 1)
    for a in range(6):
        @pl.loop(0, n - 1)
        def _(i):
            d = far_first(i)
            in_copy(a, peer(d), me, d).start()
    load_w.start()
    load_up.start()

    def in_wait(a):
        in_local(a).wait()

        @pl.loop(1, n)
        def _(d):
            in_copy(a, source(d), source(d), d).wait_recv()

    def fw_copy(i, to, owner, d):
        src, dst = ((attn_own, attn_full), (tan_own, tan_full))[i]
        return pltpu.make_async_remote_copy(
            src_ref=src.at[at(to, tok), :],
            dst_ref=dst.at[:, at(owner, hd)],
            send_sem=fw_send.at[i, d], recv_sem=fw_recv.at[i, d],
            device_id=(dp, to), device_id_type=MESH,
        )

    def fw_local(i):
        src, dst = ((attn_own, attn_full), (tan_own, tan_full))[i]
        return pltpu.make_async_copy(
            src.at[at(me, tok), :], dst.at[:, at(me, hd)], fw_recv.at[i, 0]
        )

    span = 2 * tok
    parts = n // 2

    in_wait(0)
    in_wait(1)

    @pl.loop(0, parts)
    def _(p):
        rows = at(p, span)
        s = dotf(qq[rows, hd:], kk[:, :hd], NT)
        e = jnp.exp((s - jnp.max(s, axis=1, keepdims=True)) * scale)
        inv = 1.0 / jnp.sum(e, axis=1, keepdims=True)
        inv_ref[rows, :] = inv
        e_ref[rows, :] = e
        e_low[rows, :] = e.astype(jnp.bfloat16)
        pb = (e * inv).astype(jnp.bfloat16)
        for c in range(parts):
            prob[c, rows, :] = pb[:, c * span:(c + 1) * span]

    in_wait(2)
    in_wait(3)

    @pl.loop(0, parts)
    def _(p):
        rows = at(p, span)
        wgt = e_ref[rows, :] * dotf(qq[rows, :], kk[...], NT)
        ut_ref[rows, :] = jnp.sum(wgt, axis=1, keepdims=True) * scale
        w_low[rows, :] = wgt.astype(jnp.bfloat16)

    in_wait(4)

    @pl.loop(0, parts)
    def _(p):
        rows = at(p, span)
        inv = inv_ref[rows, :]
        wide = dotf(e_low[rows, :], vv[:, :hd]) * inv
        attn_own[rows, :] = wide.astype(jnp.bfloat16)
        part = dotf(w_low[rows, :], vv[:, :hd]) * scale
        acc_ref[rows, :] = part - wide * ut_ref[rows, :]

    in_wait(5)

    @pl.loop(0, parts)
    def _(j):
        p = lax.rem(me // 2 + parts // 2 + j, parts)
        rows = at(p, span)
        acc_t = acc_ref[rows, :] + dotf(e_low[rows, :], vv[:, hd:])
        tan_own[rows, :] = (acc_t * inv_ref[rows, :]).astype(jnp.bfloat16)
        for half in range(2):
            owner = 2 * p + half
            d = lax.rem(owner + n - me, n)

            @pl.when(d != 0)
            def _():
                fw_copy(1, owner, me, d).start()

            @pl.when(d == 0)
            def _():
                fw_local(1).start()

    fw_local(0).start()

    @pl.loop(0, n - 1)
    def _(i):
        d = far_first(i)
        fw_copy(0, peer(d), me, d).start()

    load_w.wait()
    load_up.wait()

    def fw_wait(i):
        fw_local(i).wait()

        @pl.loop(1, n)
        def _(d):
            fw_copy(i, source(d), source(d), d).wait_recv()

    fw_wait(1)
    ty = dotf(tan_full[...], w_ref[...])
    tan_ref[...] = ty.astype(jnp.bfloat16)
    tan_out = pltpu.make_async_copy(tan_ref, tan_hbm, out_sem.at[0])
    block_out = pltpu.make_async_copy(block_ref, block_hbm, out_sem.at[1])
    gw_out = pltpu.make_async_copy(gw_ref, gw_hbm, out_sem.at[2])
    tan_out.start()
    cot = (ty + up_ref[...].astype(jnp.float32)).astype(jnp.bfloat16)
    cots[pl.ds(0, tok), :] = cot
    grad_loc[...] = dotf(cot, w_ref[...], NT).astype(jnp.bfloat16)

    def g_copy(to, owner, d):
        return pltpu.make_async_remote_copy(
            src_ref=grad_loc.at[:, at(to, hd)],
            dst_ref=grad_own.at[at(owner, tok), :],
            send_sem=g_send.at[d], recv_sem=g_recv.at[d],
            device_id=(dp, to), device_id_type=MESH,
        )

    g_local = pltpu.make_async_copy(
        grad_loc.at[:, at(me, hd)], grad_own.at[at(me, tok), :], g_recv.at[0]
    )
    g_local.start()

    @pl.loop(0, n - 1)
    def _(i):
        d = far_first(i)
        g_copy(peer(d), me, d).start()

    def cot_copy(src_slot, dst_slot, to):
        return pltpu.make_async_remote_copy(
            src_ref=cots.at[pl.ds(src_slot * tok, tok), :],
            dst_ref=cots.at[pl.ds(dst_slot * tok, tok), :],
            send_sem=cot_send.at[dst_slot], recv_sem=cot_recv.at[dst_slot],
            device_id=(to, me), device_id_type=MESH,
        )

    cot_x = cot_copy(0, 2, dp_peers[2])
    cot_core = cot_copy(0, 1, dp_peers[1])
    cot_fwd = cot_copy(2, 3, dp_peers[1])
    cot_x.start()
    cot_core.start()

    fw_wait(0)

    def ad_copy(j):
        return pltpu.make_async_remote_copy(
            src_ref=attn_full.at[:, at(dp_peers[j], rows_dp)],
            dst_ref=attn_dp.at[pl.ds(j * tok, tok), :],
            send_sem=ad_send.at[j], recv_sem=ad_recv.at[j],
            device_id=(dp_peers[j], me), device_id_type=MESH,
        )

    ad_local = pltpu.make_async_copy(
        attn_full.at[:, at(dp, rows_dp)], attn_dp.at[pl.ds(0, tok), :], ad_recv.at[0]
    )
    for j in range(1, ndp):
        ad_copy(j).start()
    ad_local.start()
    block_ref[...] = dotf(attn_full[...], w_ref[...]).astype(jnp.bfloat16)
    block_out.start()

    g_local.wait()

    @pl.loop(1, n)
    def _(d):
        g_copy(source(d), source(d), d).wait_recv()

    outs = ((gk_st, gk_out), (gv_st, gv_out), (gq_st, gq_out))

    def gr_copy(i, to, owner, d):
        src, dst = outs[i]
        return pltpu.make_async_remote_copy(
            src_ref=src.at[at(to, tok), :],
            dst_ref=dst.at[:, at(owner, hd)],
            send_sem=gr_send.at[i, d], recv_sem=gr_recv.at[i, d],
            device_id=(dp, to), device_id_type=MESH,
        )

    def gr_local(i):
        src, dst = outs[i]
        return pltpu.make_async_copy(
            src.at[at(me, tok), :], dst.at[:, at(me, hd)], gr_recv.at[i, 0]
        )

    g_all = grad_own[...]
    delta = jnp.sum(
        g_all.astype(jnp.float32) * attn_own[...].astype(jnp.float32), axis=1, keepdims=True
    )
    gq_acc[...] = jnp.zeros_like(gq_acc)

    def back_chunk(j):
        p = lax.rem(me // 2 + parts // 2 + j, parts)
        rows = at(p, span)
        pc = prob[p]
        dprob = dotf(g_all, vv[rows, :hd], NT)
        ds = (pc.astype(jnp.float32) * (dprob - delta)).astype(jnp.bfloat16)
        gq_acc[...] += dotf(ds, kk[rows, :hd])
        gk_st[rows, :] = (dotf(qq[:, hd:], ds, TN).T * scale).astype(jnp.bfloat16)
        gv_st[rows, :] = dotf(g_all, pc, TN).T.astype(jnp.bfloat16)
        for half in range(2):
            owner = 2 * p + half
            d = lax.rem(owner + n - me, n)

            @pl.when(d != 0)
            def _():
                gr_copy(0, owner, me, d).start()
                gr_copy(1, owner, me, d).start()

            @pl.when(d == 0)
            def _():
                gr_local(0).start()
                gr_local(1).start()

    half_n = n // 2
    spot, side = lax.rem(me, half_n), me // half_n

    def half_peer(d):
        return lax.rem(spot + d, half_n)

    def gw_copy(d):
        to = half_peer(d)
        return pltpu.make_async_remote_copy(
            src_ref=gw_st.at[:, to],
            dst_ref=gw_land.at[d],
            send_sem=gw_send.at[d], recv_sem=gw_recv.at[d],
            device_id=(dp, side * half_n + to), device_id_type=MESH,
        )

    cross = pltpu.make_async_remote_copy(
        src_ref=cross_st, dst_ref=cross_land,
        send_sem=cross_send.at[0], recv_sem=cross_recv.at[0],
        device_id=(dp, peer(half_n)), device_id_type=MESH,
    )

    first = parts // 2

    @pl.loop(0, first)
    def _(j):
        back_chunk(j)

    cot_x.wait_recv()
    cot_fwd.start()
    cot_core.wait_recv()
    ad_local.wait()
    for j in range(1, ndp):
        ad_copy(j).wait_recv()
    cot_fwd.wait_recv()
    gw_part = (dotf(attn_dp[...], cots[...], TN) * gw_scale).astype(jnp.bfloat16)
    for b in range(n):
        gw_st[b // half_n, b % half_n] = gw_part[b * rows_own:(b + 1) * rows_own, :]

    for d in range(1, half_n):
        gw_copy(d).start()

    @pl.loop(first, parts)
    def _(j):
        back_chunk(j)

    gq_st[...] = (gq_acc[...] * scale).astype(jnp.bfloat16)
    gr_local(2).start()

    @pl.loop(0, n - 1)
    def _(i):
        d = far_first(i)
        gr_copy(2, peer(d), me, d).start()

    own = gw_st[side, spot].astype(jnp.float32)
    other = gw_st[1 - side, spot].astype(jnp.float32)
    for d in range(1, half_n):
        gw_copy(d).wait_recv()
        own = own + gw_land[d, side].astype(jnp.float32)
        other = other + gw_land[d, 1 - side].astype(jnp.float32)
    cross_st[...] = other.astype(jnp.bfloat16)
    cross.start()
    cross.wait_recv()
    gw_ref[...] = own + cross_land[...].astype(jnp.float32)
    gw_out.start()

    for i in range(3):
        gr_local(i).wait()

        @pl.loop(1, n)
        def _(d):
            gr_copy(i, source(d), source(d), d).wait_recv()

    @pl.loop(1, n)
    def _(d):
        to = peer(d)
        for a in range(6):
            in_copy(a, to, me, d).wait_send()
        for i in range(2):
            fw_copy(i, to, me, d).wait_send()
        g_copy(to, me, d).wait_send()
        for i in range(3):
            gr_copy(i, to, me, d).wait_send()

    for d in range(1, half_n):
        gw_copy(d).wait_send()
    cross.wait_send()
    tan_out.wait()
    block_out.wait()
    gw_out.wait()
    cot_x.wait_send()
    cot_core.wait_send()
    cot_fwd.wait_send()
    for j in range(1, ndp):
        ad_copy(j).wait_send()


def hand_over(*refs):
    count = (len(refs) - 2) // 3
    held = refs[2 * count:3 * count]
    in_sem, out_sem = refs[-2:]
    loads = [pltpu.make_async_copy(refs[i], held[i], in_sem.at[i]) for i in range(count)]
    stores = [
        pltpu.make_async_copy(held[i], refs[count + i], out_sem.at[i]) for i in range(count)
    ]
    for load in loads:
        load.start()
    for load, store in zip(loads, stores):
        load.wait()
        store.start()
    for store in stores:
        store.wait()


def by_heads(
    queries, key_rows, value_rows, query_tangent, key_tangent, value_tangent, out_weight, upstream
):
    n, ndp = lax.axis_size("seq"), lax.axis_size("dp")
    tok, width = queries.shape[1:]
    model = out_weight.shape[1]
    full = n * tok
    hd = HEAD_DIM
    bf, f32 = jnp.bfloat16, jnp.float32
    rows_dp = width // ndp
    rows_own = rows_dp // n
    any_spec = pl.BlockSpec(memory_space=pltpu.HBM)
    dma = pltpu.SemaphoreType.DMA
    flops = 2 * full * full * hd * 10 + 8 * tok * width * model
    outs = pl.pallas_call(
        functools.partial(fused_kernel, n, ndp),
        out_shape=(
            jax.ShapeDtypeStruct((tok, model), bf),
            jax.ShapeDtypeStruct((tok, model), bf),
            jax.ShapeDtypeStruct((rows_own, model), f32),
            jax.ShapeDtypeStruct((tok, width), bf),
            jax.ShapeDtypeStruct((tok, width), bf),
            jax.ShapeDtypeStruct((tok, width), bf),
        ),
        in_specs=[any_spec] * 8,
        out_specs=(any_spec,) * 6,
        scratch_shapes=[
            pltpu.VMEM((full, 2 * hd), bf),
            pltpu.VMEM((full, 2 * hd), bf),
            pltpu.VMEM((full, 2 * hd), bf),
            pltpu.VMEM((n // 2, full, 2 * tok), bf),
            pltpu.VMEM((full, hd), bf),
            pltpu.VMEM((full, hd), bf),
            pltpu.VMEM((tok, width), bf),
            pltpu.VMEM((tok, width), bf),
            pltpu.VMEM((width, model), bf),
            pltpu.VMEM((tok, model), bf),
            pltpu.VMEM((ndp * tok, model), bf),
            pltpu.VMEM((ndp * tok, rows_dp), bf),
            pltpu.VMEM((tok, width), bf),
            pltpu.VMEM((full, hd), bf),
            pltpu.VMEM((full, hd), f32),
            pltpu.VMEM((full, hd), bf),
            pltpu.VMEM((full, hd), bf),
            pltpu.VMEM((full, hd), bf),
            pltpu.VMEM((2, n // 2, rows_own, model), bf),
            pltpu.VMEM((n // 2, 2, rows_own, model), bf),
            pltpu.VMEM((full, full), f32),
            pltpu.VMEM((full, full), bf),
            pltpu.VMEM((full, full), bf),
            pltpu.VMEM((tok, model), bf),
            pltpu.VMEM((tok, model), bf),
            pltpu.VMEM((rows_own, model), f32),
            pltpu.VMEM((rows_own, model), bf),
            pltpu.VMEM((rows_own, model), bf),
            pltpu.VMEM((full, 1), f32),
            pltpu.VMEM((full, 1), f32),
            pltpu.VMEM((full, hd), f32),
            dma((6, n)), dma((6, n)), dma((2, n)), dma((2, n)), dma((n,)), dma((n,)),
            dma((3, n)), dma((3, n)), dma((n,)), dma((n,)), dma((ndp,)), dma((ndp,)),
            dma((ndp,)), dma((ndp,)), dma((2,)),
            dma((1,)), dma((1,)), dma((3,)),
        ],
        compiler_params=pltpu.CompilerParams(
            collective_id=0, has_side_effects=True, vmem_limit_bytes=60 * 1024 * 1024
        ),
        cost_estimate=pl.CostEstimate(
            flops=flops, bytes_accessed=20 * tok * width, transcendentals=full * full
        ),
    )(
        queries[0], key_rows[0], value_rows[0], query_tangent[0], key_tangent[0],
        value_tangent[0], out_weight, upstream[0],
    )
    block, tan, gw, gq, gk, gv = pl.pallas_call(
        hand_over,
        out_shape=tuple(jax.ShapeDtypeStruct(o.shape, o.dtype) for o in outs),
        in_specs=[any_spec] * 6,
        out_specs=(any_spec,) * 6,
        scratch_shapes=[pltpu.VMEM(o.shape, o.dtype) for o in outs] + [dma((6,)), dma((6,))],
    )(*outs)
    return block[None], tan[None], gw, gq[None], gk[None], gv[None]


def solution(mesh):
    fits = mesh.shape["seq"] == HEADS and mesh.shape["dp"] == 4
    placed = (
        P("dp", "seq", None),
        P("dp", "seq", None),
        P("dp", "seq", None),
        P("dp", "seq", None),
        P("dp", "seq", None),
        P("dp", "seq", None),
        P(),
        P("dp", "seq", None),
    )
    return jax.shard_map(
        by_heads if fits else per_device,
        mesh=mesh,
        in_specs=placed,
        out_specs=(
            P("dp", "seq", None),
            P("dp", "seq", None),
            P(("dp", "seq"), None),
            P("dp", "seq", None),
            P("dp", "seq", None),
            P("dp", "seq", None),
        ),
        check_vma=False,
    )
```

```python
import functools
import math

import jax
import jax.numpy as jnp
from jax import lax
from jax.experimental import pallas as pl
from jax.experimental.pallas import tpu as pltpu
from jax.sharding import PartitionSpec as P

HEADS = 8
HEAD_DIM = 128


def to_heads(matrix):
    return matrix.reshape(matrix.shape[0], HEADS, HEAD_DIM)


def per_device(
    queries, key_rows, value_rows, query_tangent, key_tangent, value_tangent, out_weight, upstream
):
    local_q = to_heads(queries[0])
    local_tq = to_heads(query_tangent[0])
    tokens = queries.shape[1]
    attn_width = queries.shape[2]
    full_len = tokens * lax.axis_size("seq")
    softmax_scale = HEAD_DIM ** (-0.5)
    head_zeros = jnp.zeros((HEADS, tokens), jnp.float32)
    acc_zeros = jnp.zeros((tokens, HEADS, HEAD_DIM), jnp.float32)
    run_max = jnp.full((HEADS, tokens), -jnp.inf, jnp.float32)
    run_sum = head_zeros
    run_tan = head_zeros
    acc_main = acc_zeros
    acc_tan = acc_zeros
    key_piece = lax.all_gather(key_rows[0], "seq", axis=0, tiled=True)
    value_piece = lax.all_gather(value_rows[0], "seq", axis=0, tiled=True)
    key_tan_piece = lax.all_gather(key_tangent[0], "seq", axis=0, tiled=True)
    value_tan_piece = lax.all_gather(value_tangent[0], "seq", axis=0, tiled=True)
    key_heads = to_heads(key_piece)
    value_heads = to_heads(value_piece)
    key_tan_heads = to_heads(key_tan_piece)
    value_tan_heads = to_heads(value_tan_piece)
    scores = (
        jnp.einsum("thd,shd->hts", local_q, key_heads, preferred_element_type=jnp.float32)
        * softmax_scale
    )
    tan_scores = (
        jnp.einsum("thd,shd->hts", local_tq, key_heads, preferred_element_type=jnp.float32)
        + jnp.einsum("thd,shd->hts", local_q, key_tan_heads, preferred_element_type=jnp.float32)
    ) * softmax_scale
    new_max = jnp.max(scores, axis=2)
    shrink = jnp.exp(run_max - new_max)
    exp_scores = jnp.exp(scores - new_max[:, :, None])
    weighted = exp_scores * tan_scores
    run_sum = run_sum * shrink + jnp.sum(exp_scores, axis=2)
    run_tan = run_tan * shrink + jnp.sum(weighted, axis=2)
    exp_low = exp_scores.astype(jnp.bfloat16)
    weighted_low = weighted.astype(jnp.bfloat16)
    shrink_rows = shrink.T[:, :, None]
    acc_main = acc_main * shrink_rows + jnp.einsum(
        "hts,shd->thd", exp_low, value_heads, preferred_element_type=jnp.float32
    )
    acc_tan = (
        acc_tan * shrink_rows
        + jnp.einsum("hts,shd->thd", weighted_low, value_heads, preferred_element_type=jnp.float32)
        + jnp.einsum("hts,shd->thd", exp_low, value_tan_heads, preferred_element_type=jnp.float32)
    )
    key_store = key_piece
    value_store = value_piece
    folded = (new_max, run_sum, run_tan, acc_main, acc_tan, key_store, value_store)
    run_max, run_sum, run_tan, acc_main, acc_tan, key_store, value_store = folded
    sum_rows = run_sum.T[:, :, None]
    attn_wide = acc_main / sum_rows
    attn = attn_wide.astype(jnp.bfloat16)
    tan_attn = ((acc_tan - attn_wide * run_tan.T[:, :, None]) / sum_rows).astype(jnp.bfloat16)
    log_total = run_max + jnp.log(run_sum)
    attn_flat = attn.reshape(tokens, attn_width)
    tan_flat = tan_attn.reshape(tokens, attn_width)
    block_wide = jnp.dot(attn_flat, out_weight, preferred_element_type=jnp.float32)
    tan_wide = jnp.dot(tan_flat, out_weight, preferred_element_type=jnp.float32)
    cotangent = (tan_wide + upstream[0].astype(jnp.float32)).astype(jnp.bfloat16)
    grad_attn = jnp.einsum(
        "te,ke->tk", cotangent, out_weight, preferred_element_type=jnp.float32
    ).astype(jnp.bfloat16)
    grad_factor = 1.0 / math.sqrt(lax.axis_size("dp") * full_len)
    grad_heads = to_heads(grad_attn)
    row_delta = jnp.einsum("thd,thd->ht", grad_heads, attn, preferred_element_type=jnp.float32)
    key_all = to_heads(key_store)
    value_all = to_heads(value_store)
    scores_all = (
        jnp.einsum("thd,shd->hts", local_q, key_all, preferred_element_type=jnp.float32)
        * softmax_scale
    )
    attn_prob = jnp.exp(scores_all - log_total[:, :, None])
    grad_prob = jnp.einsum(
        "thd,shd->hts", grad_heads, value_all, preferred_element_type=jnp.float32
    )
    grad_scores = (attn_prob * (grad_prob - row_delta[:, :, None])).astype(jnp.bfloat16)
    grad_query = (
        softmax_scale
        * jnp.einsum("hts,shd->thd", grad_scores, key_all, preferred_element_type=jnp.float32)
    ).astype(jnp.bfloat16)
    all_lse, all_delta = (
        lax.all_gather(log_total.T, "seq", axis=0, tiled=True),
        lax.all_gather(row_delta.T, "seq", axis=0, tiled=True),
    )
    own_keys = to_heads(key_rows[0])
    own_values = to_heads(value_rows[0])
    query_piece = lax.all_gather(queries[0], "seq", axis=0, tiled=True)
    grad_piece = lax.all_gather(grad_attn, "seq", axis=0, tiled=True)
    query_heads = to_heads(query_piece)
    grad_piece_heads = to_heads(grad_piece)
    scores_piece = (
        jnp.einsum("qhd,khd->hqk", query_heads, own_keys, preferred_element_type=jnp.float32)
        * softmax_scale
    )
    prob_piece = jnp.exp(scores_piece - all_lse.T[:, :, None])
    dprob = jnp.einsum(
        "qhd,khd->hqk", grad_piece_heads, own_values, preferred_element_type=jnp.float32
    )
    dscore = (prob_piece * (dprob - all_delta.T[:, :, None])).astype(jnp.bfloat16)
    key_grad_sum = softmax_scale * jnp.einsum(
        "hqk,qhd->khd", dscore, query_heads, preferred_element_type=jnp.float32
    )
    value_grad_sum = jnp.einsum(
        "hqk,qhd->khd",
        prob_piece.astype(jnp.bfloat16),
        grad_piece_heads,
        preferred_element_type=jnp.float32,
    )
    grad_key = key_grad_sum.reshape(tokens, attn_width).astype(jnp.bfloat16)
    grad_value = value_grad_sum.reshape(tokens, attn_width).astype(jnp.bfloat16)
    grad_weight = lax.psum_scatter(
        grad_factor
        * jnp.einsum("tk,te->ke", attn_flat, cotangent, preferred_element_type=jnp.float32),
        ("dp", "seq"),
        scatter_dimension=0,
        tiled=True,
    )
    return (
        block_wide.astype(jnp.bfloat16)[None],
        tan_wide.astype(jnp.bfloat16)[None],
        grad_weight,
        grad_query.reshape(tokens, attn_width)[None],
        grad_key[None],
        grad_value[None],
    )


MESH = pl.DeviceIdType.MESH
NT = (((1,), (1,)), ((), ()))
TN = (((0,), (0,)), ((), ()))


def dotf(a, b, dims=(((1,), (0,)), ((), ()))):
    return lax.dot_general(a, b, dims, preferred_element_type=jnp.float32)


def fused_kernel(
    n, ndp, q_ref, k_ref, v_ref, tq_ref, tk_ref, tv_ref, w_hbm, up_hbm,
    block_hbm, tan_hbm, gw_hbm, gq_out, gk_out, gv_out,
    qq, kk, vv, prob, attn_own, tan_own, attn_full, tan_full, w_ref, up_ref,
    cots, attn_dp, grad_loc, grad_own, gq_acc, gq_st, gk_st, gv_st, gw_st, gw_land,
    e_ref, e_low, w_low, block_ref, tan_ref, gw_ref, cross_st, cross_land,
    inv_ref, ut_ref, acc_ref,
    in_send, in_recv, fw_send, fw_recv, g_send, g_recv, gr_send, gr_recv,
    gw_send, gw_recv, cot_send, cot_recv, ad_send, ad_recv, load_sem, cross_send, cross_recv, out_sem,
):
    dp, me = lax.axis_index("dp"), lax.axis_index("seq")
    tok = q_ref.shape[0]
    hd = HEAD_DIM
    full = n * tok
    rows_own = gw_st.shape[2]
    rows_dp = n * rows_own
    scale = HEAD_DIM ** (-0.5)
    gw_scale = 1.0 / math.sqrt(ndp * full)
    dp_peers = [dp, dp + 1 - 2 * lax.rem(dp, 2), lax.rem(dp + 2, 4), 3 - dp]

    def peer(d):
        return lax.rem(me + d, n)

    def source(d):
        return lax.rem(me + n - d, n)

    def far_first(i):
        return n // 2 + (1 - 2 * lax.rem(i, 2)) * ((i + 1) // 2)

    def at(i, size):
        return pl.ds(pl.multiple_of(i * size, size), size)

    barrier = pltpu.get_barrier_semaphore()
    for d in range(1, n):
        pl.semaphore_signal(barrier, inc=1, device_id=(dp, peer(d)), device_id_type=MESH)
    for j in range(1, ndp):
        pl.semaphore_signal(barrier, inc=1, device_id=(dp_peers[j], me), device_id_type=MESH)

    load_w = pltpu.make_async_copy(w_hbm, w_ref, load_sem.at[0])
    load_up = pltpu.make_async_copy(up_hbm, up_ref, load_sem.at[1])

    arrivals = (
        (q_ref, qq, 1), (k_ref, kk, 0), (tq_ref, qq, 0),
        (tk_ref, kk, 1), (v_ref, vv, 0), (tv_ref, vv, 1),
    )

    def in_copy(a, to, owner, d):
        src, dst, side = arrivals[a]
        return pltpu.make_async_remote_copy(
            src_ref=src.at[:, at(to, hd)],
            dst_ref=dst.at[at(owner, tok), pl.ds(side * hd, hd)],
            send_sem=in_send.at[a, d], recv_sem=in_recv.at[a, d],
            device_id=(dp, to), device_id_type=MESH,
        )

    def in_local(a):
        src, dst, side = arrivals[a]
        return pltpu.make_async_copy(
            src.at[:, at(me, hd)], dst.at[at(me, tok), pl.ds(side * hd, hd)], in_recv.at[a, 0]
        )

    for a in range(6):
        in_local(a).start()
    pl.semaphore_wait(barrier, n - 1 + ndp - 1)
    for a in range(6):
        @pl.loop(0, n - 1)
        def _(i):
            d = far_first(i)
            in_copy(a, peer(d), me, d).start()
    load_w.start()
    load_up.start()

    def in_wait(a):
        in_local(a).wait()

        @pl.loop(1, n)
        def _(d):
            in_copy(a, source(d), source(d), d).wait_recv()

    def fw_copy(i, to, owner, d):
        src, dst = ((attn_own, attn_full), (tan_own, tan_full))[i]
        return pltpu.make_async_remote_copy(
            src_ref=src.at[at(to, tok), :],
            dst_ref=dst.at[:, at(owner, hd)],
            send_sem=fw_send.at[i, d], recv_sem=fw_recv.at[i, d],
            device_id=(dp, to), device_id_type=MESH,
        )

    def fw_local(i):
        src, dst = ((attn_own, attn_full), (tan_own, tan_full))[i]
        return pltpu.make_async_copy(
            src.at[at(me, tok), :], dst.at[:, at(me, hd)], fw_recv.at[i, 0]
        )

    span = 2 * tok
    parts = n // 2

    in_wait(0)
    in_wait(1)

    @pl.loop(0, parts)
    def _(p):
        rows = at(p, span)
        s = dotf(qq[rows, hd:], kk[:, :hd], NT)
        e = jnp.exp((s - jnp.max(s, axis=1, keepdims=True)) * scale)
        inv = 1.0 / jnp.sum(e, axis=1, keepdims=True)
        inv_ref[rows, :] = inv
        e_ref[rows, :] = e
        e_low[rows, :] = e.astype(jnp.bfloat16)
        pb = (e * inv).astype(jnp.bfloat16)
        for c in range(parts):
            prob[c, rows, :] = pb[:, c * span:(c + 1) * span]

    in_wait(2)
    in_wait(3)

    @pl.loop(0, parts)
    def _(p):
        rows = at(p, span)
        wgt = e_ref[rows, :] * dotf(qq[rows, :], kk[...], NT)
        ut_ref[rows, :] = jnp.sum(wgt, axis=1, keepdims=True) * scale
        w_low[rows, :] = wgt.astype(jnp.bfloat16)

    in_wait(4)

    @pl.loop(0, parts)
    def _(p):
        rows = at(p, span)
        inv = inv_ref[rows, :]
        wide = dotf(e_low[rows, :], vv[:, :hd]) * inv
        attn_own[rows, :] = wide.astype(jnp.bfloat16)
        part = dotf(w_low[rows, :], vv[:, :hd]) * scale
        acc_ref[rows, :] = part - wide * ut_ref[rows, :]

    in_wait(5)

    @pl.loop(0, parts)
    def _(j):
        p = lax.rem(me // 2 + parts // 2 + j, parts)
        rows = at(p, span)
        acc_t = acc_ref[rows, :] + dotf(e_low[rows, :], vv[:, hd:])
        tan_own[rows, :] = (acc_t * inv_ref[rows, :]).astype(jnp.bfloat16)
        for half in range(2):
            owner = 2 * p + half
            d = lax.rem(owner + n - me, n)

            @pl.when(d != 0)
            def _():
                fw_copy(1, owner, me, d).start()

            @pl.when(d == 0)
            def _():
                fw_local(1).start()

    fw_local(0).start()

    @pl.loop(0, n - 1)
    def _(i):
        d = far_first(i)
        fw_copy(0, peer(d), me, d).start()

    load_w.wait()
    load_up.wait()

    def fw_wait(i):
        fw_local(i).wait()

        @pl.loop(1, n)
        def _(d):
            fw_copy(i, source(d), source(d), d).wait_recv()

    fw_wait(1)
    ty = dotf(tan_full[...], w_ref[...])
    tan_ref[...] = ty.astype(jnp.bfloat16)
    tan_out = pltpu.make_async_copy(tan_ref, tan_hbm, out_sem.at[0])
    block_out = pltpu.make_async_copy(block_ref, block_hbm, out_sem.at[1])
    gw_out = pltpu.make_async_copy(gw_ref, gw_hbm, out_sem.at[2])
    tan_out.start()
    cot = (ty + up_ref[...].astype(jnp.float32)).astype(jnp.bfloat16)
    cots[pl.ds(0, tok), :] = cot

    def cot_copy(src_slot, dst_slot, to):
        return pltpu.make_async_remote_copy(
            src_ref=cots.at[pl.ds(src_slot * tok, tok), :],
            dst_ref=cots.at[pl.ds(dst_slot * tok, tok), :],
            send_sem=cot_send.at[dst_slot], recv_sem=cot_recv.at[dst_slot],
            device_id=(to, me), device_id_type=MESH,
        )

    cot_x = cot_copy(0, 2, dp_peers[2])
    cot_core = cot_copy(0, 1, dp_peers[1])
    cot_fwd = cot_copy(2, 3, dp_peers[1])
    cot_x.start()
    cot_core.start()

    grad_loc[...] = dotf(cot, w_ref[...], NT).astype(jnp.bfloat16)

    def g_copy(to, owner, d):
        return pltpu.make_async_remote_copy(
            src_ref=grad_loc.at[:, at(to, hd)],
            dst_ref=grad_own.at[at(owner, tok), :],
            send_sem=g_send.at[d], recv_sem=g_recv.at[d],
            device_id=(dp, to), device_id_type=MESH,
        )

    g_local = pltpu.make_async_copy(
        grad_loc.at[:, at(me, hd)], grad_own.at[at(me, tok), :], g_recv.at[0]
    )
    g_local.start()

    @pl.loop(0, n - 1)
    def _(i):
        d = far_first(i)
        g_copy(peer(d), me, d).start()

    fw_wait(0)

    def ad_copy(j):
        return pltpu.make_async_remote_copy(
            src_ref=attn_full.at[:, at(dp_peers[j], rows_dp)],
            dst_ref=attn_dp.at[pl.ds(j * tok, tok), :],
            send_sem=ad_send.at[j], recv_sem=ad_recv.at[j],
            device_id=(dp_peers[j], me), device_id_type=MESH,
        )

    ad_local = pltpu.make_async_copy(
        attn_full.at[:, at(dp, rows_dp)], attn_dp.at[pl.ds(0, tok), :], ad_recv.at[0]
    )
    for j in range(1, ndp):
        ad_copy(j).start()
    ad_local.start()
    block_ref[...] = dotf(attn_full[...], w_ref[...]).astype(jnp.bfloat16)
    block_out.start()

    g_local.wait()

    @pl.loop(1, n)
    def _(d):
        g_copy(source(d), source(d), d).wait_recv()

    outs = ((gk_st, gk_out), (gv_st, gv_out), (gq_st, gq_out))

    def gr_copy(i, to, owner, d):
        src, dst = outs[i]
        return pltpu.make_async_remote_copy(
            src_ref=src.at[at(to, tok), :],
            dst_ref=dst.at[:, at(owner, hd)],
            send_sem=gr_send.at[i, d], recv_sem=gr_recv.at[i, d],
            device_id=(dp, to), device_id_type=MESH,
        )

    def gr_local(i):
        src, dst = outs[i]
        return pltpu.make_async_copy(
            src.at[at(me, tok), :], dst.at[:, at(me, hd)], gr_recv.at[i, 0]
        )

    g_all = grad_own[...]
    delta = jnp.sum(
        g_all.astype(jnp.float32) * attn_own[...].astype(jnp.float32), axis=1, keepdims=True
    )
    gq_acc[...] = jnp.zeros_like(gq_acc)

    def back_chunk(j):
        p = lax.rem(me // 2 + parts // 2 + j, parts)
        rows = at(p, span)
        pc = prob[p]
        dprob = dotf(g_all, vv[rows, :hd], NT)
        ds = (pc.astype(jnp.float32) * (dprob - delta)).astype(jnp.bfloat16)
        gq_acc[...] += dotf(ds, kk[rows, :hd])
        gk_st[rows, :] = (dotf(qq[:, hd:], ds, TN).T * scale).astype(jnp.bfloat16)
        gv_st[rows, :] = dotf(g_all, pc, TN).T.astype(jnp.bfloat16)
        for half in range(2):
            owner = 2 * p + half
            d = lax.rem(owner + n - me, n)

            @pl.when(d != 0)
            def _():
                gr_copy(0, owner, me, d).start()
                gr_copy(1, owner, me, d).start()

            @pl.when(d == 0)
            def _():
                gr_local(0).start()
                gr_local(1).start()

    half_n = n // 2
    spot, side = lax.rem(me, half_n), me // half_n

    def half_peer(d):
        return lax.rem(spot + d, half_n)

    def gw_copy(d):
        to = half_peer(d)
        return pltpu.make_async_remote_copy(
            src_ref=gw_st.at[:, to],
            dst_ref=gw_land.at[d],
            send_sem=gw_send.at[d], recv_sem=gw_recv.at[d],
            device_id=(dp, side * half_n + to), device_id_type=MESH,
        )

    cross = pltpu.make_async_remote_copy(
        src_ref=cross_st, dst_ref=cross_land,
        send_sem=cross_send.at[0], recv_sem=cross_recv.at[0],
        device_id=(dp, peer(half_n)), device_id_type=MESH,
    )

    first = parts // 2

    @pl.loop(0, first)
    def _(j):
        back_chunk(j)

    cot_x.wait_recv()
    cot_fwd.start()
    cot_core.wait_recv()
    ad_local.wait()
    for j in range(1, ndp):
        ad_copy(j).wait_recv()
    cot_fwd.wait_recv()
    gw_part = (dotf(attn_dp[...], cots[...], TN) * gw_scale).astype(jnp.bfloat16)
    for b in range(n):
        gw_st[b // half_n, b % half_n] = gw_part[b * rows_own:(b + 1) * rows_own, :]

    for d in range(1, half_n):
        gw_copy(d).start()

    @pl.loop(first, parts)
    def _(j):
        back_chunk(j)

    gq_st[...] = (gq_acc[...] * scale).astype(jnp.bfloat16)
    gr_local(2).start()

    @pl.loop(0, n - 1)
    def _(i):
        d = far_first(i)
        gr_copy(2, peer(d), me, d).start()

    own = gw_st[side, spot].astype(jnp.float32)
    other = gw_st[1 - side, spot].astype(jnp.float32)
    for d in range(1, half_n):
        gw_copy(d).wait_recv()
        own = own + gw_land[d, side].astype(jnp.float32)
        other = other + gw_land[d, 1 - side].astype(jnp.float32)
    cross_st[...] = other.astype(jnp.bfloat16)
    cross.start()
    cross.wait_recv()
    gw_ref[...] = own + cross_land[...].astype(jnp.float32)
    gw_out.start()

    for i in range(3):
        gr_local(i).wait()

        @pl.loop(1, n)
        def _(d):
            gr_copy(i, source(d), source(d), d).wait_recv()

    @pl.loop(1, n)
    def _(d):
        to = peer(d)
        for a in range(6):
            in_copy(a, to, me, d).wait_send()
        for i in range(2):
            fw_copy(i, to, me, d).wait_send()
        g_copy(to, me, d).wait_send()
        for i in range(3):
            gr_copy(i, to, me, d).wait_send()

    for d in range(1, half_n):
        gw_copy(d).wait_send()
    cross.wait_send()
    tan_out.wait()
    block_out.wait()
    gw_out.wait()
    cot_x.wait_send()
    cot_core.wait_send()
    cot_fwd.wait_send()
    for j in range(1, ndp):
        ad_copy(j).wait_send()


def hand_over(*refs):
    count = (len(refs) - 2) // 3
    held = refs[2 * count:3 * count]
    in_sem, out_sem = refs[-2:]
    loads = [pltpu.make_async_copy(refs[i], held[i], in_sem.at[i]) for i in range(count)]
    stores = [
        pltpu.make_async_copy(held[i], refs[count + i], out_sem.at[i]) for i in range(count)
    ]
    for load in loads:
        load.start()
    for load, store in zip(loads, stores):
        load.wait()
        store.start()
    for store in stores:
        store.wait()


def by_heads(
    queries, key_rows, value_rows, query_tangent, key_tangent, value_tangent, out_weight, upstream
):
    n, ndp = lax.axis_size("seq"), lax.axis_size("dp")
    tok, width = queries.shape[1:]
    model = out_weight.shape[1]
    full = n * tok
    hd = HEAD_DIM
    bf, f32 = jnp.bfloat16, jnp.float32
    rows_dp = width // ndp
    rows_own = rows_dp // n
    any_spec = pl.BlockSpec(memory_space=pltpu.HBM)
    dma = pltpu.SemaphoreType.DMA
    flops = 2 * full * full * hd * 10 + 8 * tok * width * model
    outs = pl.pallas_call(
        functools.partial(fused_kernel, n, ndp),
        out_shape=(
            jax.ShapeDtypeStruct((tok, model), bf),
            jax.ShapeDtypeStruct((tok, model), bf),
            jax.ShapeDtypeStruct((rows_own, model), f32),
            jax.ShapeDtypeStruct((tok, width), bf),
            jax.ShapeDtypeStruct((tok, width), bf),
            jax.ShapeDtypeStruct((tok, width), bf),
        ),
        in_specs=[any_spec] * 8,
        out_specs=(any_spec,) * 6,
        scratch_shapes=[
            pltpu.VMEM((full, 2 * hd), bf),
            pltpu.VMEM((full, 2 * hd), bf),
            pltpu.VMEM((full, 2 * hd), bf),
            pltpu.VMEM((n // 2, full, 2 * tok), bf),
            pltpu.VMEM((full, hd), bf),
            pltpu.VMEM((full, hd), bf),
            pltpu.VMEM((tok, width), bf),
            pltpu.VMEM((tok, width), bf),
            pltpu.VMEM((width, model), bf),
            pltpu.VMEM((tok, model), bf),
            pltpu.VMEM((ndp * tok, model), bf),
            pltpu.VMEM((ndp * tok, rows_dp), bf),
            pltpu.VMEM((tok, width), bf),
            pltpu.VMEM((full, hd), bf),
            pltpu.VMEM((full, hd), f32),
            pltpu.VMEM((full, hd), bf),
            pltpu.VMEM((full, hd), bf),
            pltpu.VMEM((full, hd), bf),
            pltpu.VMEM((2, n // 2, rows_own, model), bf),
            pltpu.VMEM((n // 2, 2, rows_own, model), bf),
            pltpu.VMEM((full, full), f32),
            pltpu.VMEM((full, full), bf),
            pltpu.VMEM((full, full), bf),
            pltpu.VMEM((tok, model), bf),
            pltpu.VMEM((tok, model), bf),
            pltpu.VMEM((rows_own, model), f32),
            pltpu.VMEM((rows_own, model), bf),
            pltpu.VMEM((rows_own, model), bf),
            pltpu.VMEM((full, 1), f32),
            pltpu.VMEM((full, 1), f32),
            pltpu.VMEM((full, hd), f32),
            dma((6, n)), dma((6, n)), dma((2, n)), dma((2, n)), dma((n,)), dma((n,)),
            dma((3, n)), dma((3, n)), dma((n,)), dma((n,)), dma((ndp,)), dma((ndp,)),
            dma((ndp,)), dma((ndp,)), dma((2,)),
            dma((1,)), dma((1,)), dma((3,)),
        ],
        compiler_params=pltpu.CompilerParams(
            collective_id=0, has_side_effects=True, vmem_limit_bytes=60 * 1024 * 1024
        ),
        cost_estimate=pl.CostEstimate(
            flops=flops, bytes_accessed=20 * tok * width, transcendentals=full * full
        ),
    )(
        queries[0], key_rows[0], value_rows[0], query_tangent[0], key_tangent[0],
        value_tangent[0], out_weight, upstream[0],
    )
    block, tan, gw, gq, gk, gv = pl.pallas_call(
        hand_over,
        out_shape=tuple(jax.ShapeDtypeStruct(o.shape, o.dtype) for o in outs),
        in_specs=[any_spec] * 6,
        out_specs=(any_spec,) * 6,
        scratch_shapes=[pltpu.VMEM(o.shape, o.dtype) for o in outs] + [dma((6,)), dma((6,))],
    )(*outs)
    return block[None], tan[None], gw, gq[None], gk[None], gv[None]


def solution(mesh):
    fits = mesh.shape["seq"] == HEADS and mesh.shape["dp"] == 4
    placed = (
        P("dp", "seq", None),
        P("dp", "seq", None),
        P("dp", "seq", None),
        P("dp", "seq", None),
        P("dp", "seq", None),
        P("dp", "seq", None),
        P(),
        P("dp", "seq", None),
    )
    return jax.shard_map(
        by_heads if fits else per_device,
        mesh=mesh,
        in_specs=placed,
        out_specs=(
            P("dp", "seq", None),
            P("dp", "seq", None),
            P(("dp", "seq"), None),
            P("dp", "seq", None),
            P("dp", "seq", None),
            P("dp", "seq", None),
        ),
        check_vma=False,
    )
```

```python
import functools
import math

import jax
import jax.numpy as jnp
from jax import lax
from jax.experimental import pallas as pl
from jax.experimental.pallas import tpu as pltpu
from jax.sharding import PartitionSpec as P

HEADS = 8
HEAD_DIM = 128


def to_heads(matrix):
    return matrix.reshape(matrix.shape[0], HEADS, HEAD_DIM)


def per_device(
    queries, key_rows, value_rows, query_tangent, key_tangent, value_tangent, out_weight, upstream
):
    local_q = to_heads(queries[0])
    local_tq = to_heads(query_tangent[0])
    tokens = queries.shape[1]
    attn_width = queries.shape[2]
    full_len = tokens * lax.axis_size("seq")
    softmax_scale = HEAD_DIM ** (-0.5)
    head_zeros = jnp.zeros((HEADS, tokens), jnp.float32)
    acc_zeros = jnp.zeros((tokens, HEADS, HEAD_DIM), jnp.float32)
    run_max = jnp.full((HEADS, tokens), -jnp.inf, jnp.float32)
    run_sum = head_zeros
    run_tan = head_zeros
    acc_main = acc_zeros
    acc_tan = acc_zeros
    key_piece = lax.all_gather(key_rows[0], "seq", axis=0, tiled=True)
    value_piece = lax.all_gather(value_rows[0], "seq", axis=0, tiled=True)
    key_tan_piece = lax.all_gather(key_tangent[0], "seq", axis=0, tiled=True)
    value_tan_piece = lax.all_gather(value_tangent[0], "seq", axis=0, tiled=True)
    key_heads = to_heads(key_piece)
    value_heads = to_heads(value_piece)
    key_tan_heads = to_heads(key_tan_piece)
    value_tan_heads = to_heads(value_tan_piece)
    scores = (
        jnp.einsum("thd,shd->hts", local_q, key_heads, preferred_element_type=jnp.float32)
        * softmax_scale
    )
    tan_scores = (
        jnp.einsum("thd,shd->hts", local_tq, key_heads, preferred_element_type=jnp.float32)
        + jnp.einsum("thd,shd->hts", local_q, key_tan_heads, preferred_element_type=jnp.float32)
    ) * softmax_scale
    new_max = jnp.max(scores, axis=2)
    shrink = jnp.exp(run_max - new_max)
    exp_scores = jnp.exp(scores - new_max[:, :, None])
    weighted = exp_scores * tan_scores
    run_sum = run_sum * shrink + jnp.sum(exp_scores, axis=2)
    run_tan = run_tan * shrink + jnp.sum(weighted, axis=2)
    exp_low = exp_scores.astype(jnp.bfloat16)
    weighted_low = weighted.astype(jnp.bfloat16)
    shrink_rows = shrink.T[:, :, None]
    acc_main = acc_main * shrink_rows + jnp.einsum(
        "hts,shd->thd", exp_low, value_heads, preferred_element_type=jnp.float32
    )
    acc_tan = (
        acc_tan * shrink_rows
        + jnp.einsum("hts,shd->thd", weighted_low, value_heads, preferred_element_type=jnp.float32)
        + jnp.einsum("hts,shd->thd", exp_low, value_tan_heads, preferred_element_type=jnp.float32)
    )
    key_store = key_piece
    value_store = value_piece
    folded = (new_max, run_sum, run_tan, acc_main, acc_tan, key_store, value_store)
    run_max, run_sum, run_tan, acc_main, acc_tan, key_store, value_store = folded
    sum_rows = run_sum.T[:, :, None]
    attn_wide = acc_main / sum_rows
    attn = attn_wide.astype(jnp.bfloat16)
    tan_attn = ((acc_tan - attn_wide * run_tan.T[:, :, None]) / sum_rows).astype(jnp.bfloat16)
    log_total = run_max + jnp.log(run_sum)
    attn_flat = attn.reshape(tokens, attn_width)
    tan_flat = tan_attn.reshape(tokens, attn_width)
    block_wide = jnp.dot(attn_flat, out_weight, preferred_element_type=jnp.float32)
    tan_wide = jnp.dot(tan_flat, out_weight, preferred_element_type=jnp.float32)
    cotangent = (tan_wide + upstream[0].astype(jnp.float32)).astype(jnp.bfloat16)
    grad_attn = jnp.einsum(
        "te,ke->tk", cotangent, out_weight, preferred_element_type=jnp.float32
    ).astype(jnp.bfloat16)
    grad_factor = 1.0 / math.sqrt(lax.axis_size("dp") * full_len)
    grad_heads = to_heads(grad_attn)
    row_delta = jnp.einsum("thd,thd->ht", grad_heads, attn, preferred_element_type=jnp.float32)
    key_all = to_heads(key_store)
    value_all = to_heads(value_store)
    scores_all = (
        jnp.einsum("thd,shd->hts", local_q, key_all, preferred_element_type=jnp.float32)
        * softmax_scale
    )
    attn_prob = jnp.exp(scores_all - log_total[:, :, None])
    grad_prob = jnp.einsum(
        "thd,shd->hts", grad_heads, value_all, preferred_element_type=jnp.float32
    )
    grad_scores = (attn_prob * (grad_prob - row_delta[:, :, None])).astype(jnp.bfloat16)
    grad_query = (
        softmax_scale
        * jnp.einsum("hts,shd->thd", grad_scores, key_all, preferred_element_type=jnp.float32)
    ).astype(jnp.bfloat16)
    all_lse, all_delta = (
        lax.all_gather(log_total.T, "seq", axis=0, tiled=True),
        lax.all_gather(row_delta.T, "seq", axis=0, tiled=True),
    )
    own_keys = to_heads(key_rows[0])
    own_values = to_heads(value_rows[0])
    query_piece = lax.all_gather(queries[0], "seq", axis=0, tiled=True)
    grad_piece = lax.all_gather(grad_attn, "seq", axis=0, tiled=True)
    query_heads = to_heads(query_piece)
    grad_piece_heads = to_heads(grad_piece)
    scores_piece = (
        jnp.einsum("qhd,khd->hqk", query_heads, own_keys, preferred_element_type=jnp.float32)
        * softmax_scale
    )
    prob_piece = jnp.exp(scores_piece - all_lse.T[:, :, None])
    dprob = jnp.einsum(
        "qhd,khd->hqk", grad_piece_heads, own_values, preferred_element_type=jnp.float32
    )
    dscore = (prob_piece * (dprob - all_delta.T[:, :, None])).astype(jnp.bfloat16)
    key_grad_sum = softmax_scale * jnp.einsum(
        "hqk,qhd->khd", dscore, query_heads, preferred_element_type=jnp.float32
    )
    value_grad_sum = jnp.einsum(
        "hqk,qhd->khd",
        prob_piece.astype(jnp.bfloat16),
        grad_piece_heads,
        preferred_element_type=jnp.float32,
    )
    grad_key = key_grad_sum.reshape(tokens, attn_width).astype(jnp.bfloat16)
    grad_value = value_grad_sum.reshape(tokens, attn_width).astype(jnp.bfloat16)
    grad_weight = lax.psum_scatter(
        grad_factor
        * jnp.einsum("tk,te->ke", attn_flat, cotangent, preferred_element_type=jnp.float32),
        ("dp", "seq"),
        scatter_dimension=0,
        tiled=True,
    )
    return (
        block_wide.astype(jnp.bfloat16)[None],
        tan_wide.astype(jnp.bfloat16)[None],
        grad_weight,
        grad_query.reshape(tokens, attn_width)[None],
        grad_key[None],
        grad_value[None],
    )


MESH = pl.DeviceIdType.MESH
NT = (((1,), (1,)), ((), ()))
TN = (((0,), (0,)), ((), ()))


def dotf(a, b, dims=(((1,), (0,)), ((), ()))):
    return lax.dot_general(a, b, dims, preferred_element_type=jnp.float32)


def fused_kernel(
    n, ndp, q_ref, k_ref, v_ref, tq_ref, tk_ref, tv_ref, w_hbm, up_hbm,
    block_hbm, tan_hbm, gw_hbm, gq_out, gk_out, gv_out,
    qq, kk, vv, prob, attn_own, tan_own, attn_full, tan_full, w_ref, up_ref,
    cots, attn_dp, grad_loc, grad_own, gq_acc, gq_st, gk_st, gv_st, gw_st, gw_land,
    e_ref, e_low, w_low, block_ref, tan_ref, gw_ref, cross_st, cross_land,
    inv_ref, ut_ref, acc_ref,
    in_send, in_recv, fw_send, fw_recv, g_send, g_recv, gr_send, gr_recv,
    gw_send, gw_recv, cot_send, cot_recv, ad_send, ad_recv, load_sem, cross_send, cross_recv, out_sem,
):
    dp, me = lax.axis_index("dp"), lax.axis_index("seq")
    tok = q_ref.shape[0]
    hd = HEAD_DIM
    full = n * tok
    rows_own = gw_st.shape[2]
    rows_dp = n * rows_own
    scale = HEAD_DIM ** (-0.5)
    gw_scale = 1.0 / math.sqrt(ndp * full)
    dp_peers = [dp, dp + 1 - 2 * lax.rem(dp, 2), lax.rem(dp + 2, 4), 3 - dp]

    def peer(d):
        return lax.rem(me + d, n)

    def source(d):
        return lax.rem(me + n - d, n)

    def far_first(i):
        return n // 2 + (1 - 2 * lax.rem(i, 2)) * ((i + 1) // 2)

    def at(i, size):
        return pl.ds(pl.multiple_of(i * size, size), size)

    barrier = pltpu.get_barrier_semaphore()
    for d in range(1, n):
        pl.semaphore_signal(barrier, inc=1, device_id=(dp, peer(d)), device_id_type=MESH)
    for j in range(1, ndp):
        pl.semaphore_signal(barrier, inc=1, device_id=(dp_peers[j], me), device_id_type=MESH)

    load_w = pltpu.make_async_copy(w_hbm, w_ref, load_sem.at[0])
    load_up = pltpu.make_async_copy(up_hbm, up_ref, load_sem.at[1])

    arrivals = (
        (q_ref, qq, 1), (k_ref, kk, 0), (tq_ref, qq, 0),
        (tk_ref, kk, 1), (v_ref, vv, 0), (tv_ref, vv, 1),
    )

    def in_copy(a, to, owner, d):
        src, dst, side = arrivals[a]
        return pltpu.make_async_remote_copy(
            src_ref=src.at[:, at(to, hd)],
            dst_ref=dst.at[at(owner, tok), pl.ds(side * hd, hd)],
            send_sem=in_send.at[a, d], recv_sem=in_recv.at[a, d],
            device_id=(dp, to), device_id_type=MESH,
        )

    def in_local(a):
        src, dst, side = arrivals[a]
        return pltpu.make_async_copy(
            src.at[:, at(me, hd)], dst.at[at(me, tok), pl.ds(side * hd, hd)], in_recv.at[a, 0]
        )

    for a in range(6):
        in_local(a).start()
    pl.semaphore_wait(barrier, n - 1 + ndp - 1)
    for a in range(6):
        @pl.loop(0, n - 1)
        def _(i):
            d = far_first(i)
            in_copy(a, peer(d), me, d).start()
    load_w.start()
    load_up.start()

    def in_wait(a):
        in_local(a).wait()

        @pl.loop(1, n)
        def _(d):
            in_copy(a, source(d), source(d), d).wait_recv()

    def fw_copy(i, to, owner, d):
        src, dst = ((attn_own, attn_full), (tan_own, tan_full))[i]
        return pltpu.make_async_remote_copy(
            src_ref=src.at[at(to, tok), :],
            dst_ref=dst.at[:, at(owner, hd)],
            send_sem=fw_send.at[i, d], recv_sem=fw_recv.at[i, d],
            device_id=(dp, to), device_id_type=MESH,
        )

    def fw_local(i):
        src, dst = ((attn_own, attn_full), (tan_own, tan_full))[i]
        return pltpu.make_async_copy(
            src.at[at(me, tok), :], dst.at[:, at(me, hd)], fw_recv.at[i, 0]
        )

    span = 2 * tok
    parts = n // 2

    in_wait(0)
    in_wait(1)

    @pl.loop(0, parts)
    def _(p):
        rows = at(p, span)
        s = dotf(qq[rows, hd:], kk[:, :hd], NT)
        e = jnp.exp((s - jnp.max(s, axis=1, keepdims=True)) * scale)
        inv = 1.0 / jnp.sum(e, axis=1, keepdims=True)
        inv_ref[rows, :] = inv
        e_ref[rows, :] = e
        e_low[rows, :] = e.astype(jnp.bfloat16)
        pb = (e * inv).astype(jnp.bfloat16)
        for c in range(parts):
            prob[c, rows, :] = pb[:, c * span:(c + 1) * span]

    in_wait(2)
    in_wait(3)

    @pl.loop(0, parts)
    def _(p):
        rows = at(p, span)
        wgt = e_ref[rows, :] * dotf(qq[rows, :], kk[...], NT)
        ut_ref[rows, :] = jnp.sum(wgt, axis=1, keepdims=True) * scale
        w_low[rows, :] = wgt.astype(jnp.bfloat16)

    in_wait(4)

    @pl.loop(0, parts)
    def _(p):
        rows = at(p, span)
        inv = inv_ref[rows, :]
        wide = dotf(e_low[rows, :], vv[:, :hd]) * inv
        attn_own[rows, :] = wide.astype(jnp.bfloat16)
        part = dotf(w_low[rows, :], vv[:, :hd]) * scale
        acc_ref[rows, :] = part - wide * ut_ref[rows, :]

    in_wait(5)

    @pl.loop(0, parts)
    def _(j):
        p = lax.rem(me // 2 + parts // 2 + j, parts)
        rows = at(p, span)
        acc_t = acc_ref[rows, :] + dotf(e_low[rows, :], vv[:, hd:])
        tan_own[rows, :] = (acc_t * inv_ref[rows, :]).astype(jnp.bfloat16)
        for half in range(2):
            owner = 2 * p + half
            d = lax.rem(owner + n - me, n)

            @pl.when(d != 0)
            def _():
                fw_copy(1, owner, me, d).start()

            @pl.when(d == 0)
            def _():
                fw_local(1).start()

    load_w.wait()
    load_up.wait()

    def fw_wait(i):
        fw_local(i).wait()

        @pl.loop(1, n)
        def _(d):
            fw_copy(i, source(d), source(d), d).wait_recv()

    fw_wait(1)
    fw_local(0).start()

    @pl.loop(0, n - 1)
    def _(i):
        d = far_first(i)
        fw_copy(0, peer(d), me, d).start()

    ty = dotf(tan_full[...], w_ref[...])
    tan_ref[...] = ty.astype(jnp.bfloat16)
    tan_out = pltpu.make_async_copy(tan_ref, tan_hbm, out_sem.at[0])
    block_out = pltpu.make_async_copy(block_ref, block_hbm, out_sem.at[1])
    gw_out = pltpu.make_async_copy(gw_ref, gw_hbm, out_sem.at[2])
    tan_out.start()
    cot = (ty + up_ref[...].astype(jnp.float32)).astype(jnp.bfloat16)
    cots[pl.ds(0, tok), :] = cot

    def cot_copy(src_slot, dst_slot, to):
        return pltpu.make_async_remote_copy(
            src_ref=cots.at[pl.ds(src_slot * tok, tok), :],
            dst_ref=cots.at[pl.ds(dst_slot * tok, tok), :],
            send_sem=cot_send.at[dst_slot], recv_sem=cot_recv.at[dst_slot],
            device_id=(to, me), device_id_type=MESH,
        )

    cot_x = cot_copy(0, 2, dp_peers[2])
    cot_core = cot_copy(0, 1, dp_peers[1])
    cot_fwd = cot_copy(2, 3, dp_peers[1])
    cot_x.start()
    cot_core.start()

    grad_loc[...] = dotf(cot, w_ref[...], NT).astype(jnp.bfloat16)

    def g_copy(to, owner, d):
        return pltpu.make_async_remote_copy(
            src_ref=grad_loc.at[:, at(to, hd)],
            dst_ref=grad_own.at[at(owner, tok), :],
            send_sem=g_send.at[d], recv_sem=g_recv.at[d],
            device_id=(dp, to), device_id_type=MESH,
        )

    g_local = pltpu.make_async_copy(
        grad_loc.at[:, at(me, hd)], grad_own.at[at(me, tok), :], g_recv.at[0]
    )
    g_local.start()

    @pl.loop(0, n - 1)
    def _(i):
        d = far_first(i)
        g_copy(peer(d), me, d).start()

    fw_wait(0)

    def ad_copy(j):
        return pltpu.make_async_remote_copy(
            src_ref=attn_full.at[:, at(dp_peers[j], rows_dp)],
            dst_ref=attn_dp.at[pl.ds(j * tok, tok), :],
            send_sem=ad_send.at[j], recv_sem=ad_recv.at[j],
            device_id=(dp_peers[j], me), device_id_type=MESH,
        )

    ad_local = pltpu.make_async_copy(
        attn_full.at[:, at(dp, rows_dp)], attn_dp.at[pl.ds(0, tok), :], ad_recv.at[0]
    )
    for j in range(1, ndp):
        ad_copy(j).start()
    ad_local.start()
    block_ref[...] = dotf(attn_full[...], w_ref[...]).astype(jnp.bfloat16)
    block_out.start()

    g_local.wait()

    @pl.loop(1, n)
    def _(d):
        g_copy(source(d), source(d), d).wait_recv()

    outs = ((gk_st, gk_out), (gv_st, gv_out), (gq_st, gq_out))

    def gr_copy(i, to, owner, d):
        src, dst = outs[i]
        return pltpu.make_async_remote_copy(
            src_ref=src.at[at(to, tok), :],
            dst_ref=dst.at[:, at(owner, hd)],
            send_sem=gr_send.at[i, d], recv_sem=gr_recv.at[i, d],
            device_id=(dp, to), device_id_type=MESH,
        )

    def gr_local(i):
        src, dst = outs[i]
        return pltpu.make_async_copy(
            src.at[at(me, tok), :], dst.at[:, at(me, hd)], gr_recv.at[i, 0]
        )

    g_all = grad_own[...]
    delta = jnp.sum(
        g_all.astype(jnp.float32) * attn_own[...].astype(jnp.float32), axis=1, keepdims=True
    )
    gq_acc[...] = jnp.zeros_like(gq_acc)

    def back_chunk(j):
        p = lax.rem(me // 2 + parts // 2 + j, parts)
        rows = at(p, span)
        pc = prob[p]
        dprob = dotf(g_all, vv[rows, :hd], NT)
        ds = (pc.astype(jnp.float32) * (dprob - delta)).astype(jnp.bfloat16)
        gq_acc[...] += dotf(ds, kk[rows, :hd])
        gk_st[rows, :] = (dotf(qq[:, hd:], ds, TN).T * scale).astype(jnp.bfloat16)
        gv_st[rows, :] = dotf(g_all, pc, TN).T.astype(jnp.bfloat16)
        for half in range(2):
            owner = 2 * p + half
            d = lax.rem(owner + n - me, n)

            @pl.when(d != 0)
            def _():
                gr_copy(0, owner, me, d).start()
                gr_copy(1, owner, me, d).start()

            @pl.when(d == 0)
            def _():
                gr_local(0).start()
                gr_local(1).start()

    half_n = n // 2
    spot, side = lax.rem(me, half_n), me // half_n

    def half_peer(d):
        return lax.rem(spot + d, half_n)

    def gw_copy(d):
        to = half_peer(d)
        return pltpu.make_async_remote_copy(
            src_ref=gw_st.at[:, to],
            dst_ref=gw_land.at[d],
            send_sem=gw_send.at[d], recv_sem=gw_recv.at[d],
            device_id=(dp, side * half_n + to), device_id_type=MESH,
        )

    cross = pltpu.make_async_remote_copy(
        src_ref=cross_st, dst_ref=cross_land,
        send_sem=cross_send.at[0], recv_sem=cross_recv.at[0],
        device_id=(dp, peer(half_n)), device_id_type=MESH,
    )

    first = parts // 2

    @pl.loop(0, first)
    def _(j):
        back_chunk(j)

    cot_x.wait_recv()
    cot_fwd.start()
    cot_core.wait_recv()
    ad_local.wait()
    for j in range(1, ndp):
        ad_copy(j).wait_recv()
    cot_fwd.wait_recv()
    gw_part = (dotf(attn_dp[...], cots[...], TN) * gw_scale).astype(jnp.bfloat16)
    for b in range(n):
        gw_st[b // half_n, b % half_n] = gw_part[b * rows_own:(b + 1) * rows_own, :]

    for d in range(1, half_n):
        gw_copy(d).start()

    @pl.loop(first, parts)
    def _(j):
        back_chunk(j)

    gq_st[...] = (gq_acc[...] * scale).astype(jnp.bfloat16)
    gr_local(2).start()

    @pl.loop(0, n - 1)
    def _(i):
        d = far_first(i)
        gr_copy(2, peer(d), me, d).start()

    own = gw_st[side, spot].astype(jnp.float32)
    other = gw_st[1 - side, spot].astype(jnp.float32)
    for d in range(1, half_n):
        gw_copy(d).wait_recv()
        own = own + gw_land[d, side].astype(jnp.float32)
        other = other + gw_land[d, 1 - side].astype(jnp.float32)
    cross_st[...] = other.astype(jnp.bfloat16)
    cross.start()
    cross.wait_recv()
    gw_ref[...] = own + cross_land[...].astype(jnp.float32)
    gw_out.start()

    for i in range(3):
        gr_local(i).wait()

        @pl.loop(1, n)
        def _(d):
            gr_copy(i, source(d), source(d), d).wait_recv()

    @pl.loop(1, n)
    def _(d):
        to = peer(d)
        for a in range(6):
            in_copy(a, to, me, d).wait_send()
        for i in range(2):
            fw_copy(i, to, me, d).wait_send()
        g_copy(to, me, d).wait_send()
        for i in range(3):
            gr_copy(i, to, me, d).wait_send()

    for d in range(1, half_n):
        gw_copy(d).wait_send()
    cross.wait_send()
    tan_out.wait()
    block_out.wait()
    gw_out.wait()
    cot_x.wait_send()
    cot_core.wait_send()
    cot_fwd.wait_send()
    for j in range(1, ndp):
        ad_copy(j).wait_send()


def hand_over(*refs):
    count = (len(refs) - 2) // 3
    held = refs[2 * count:3 * count]
    in_sem, out_sem = refs[-2:]
    loads = [pltpu.make_async_copy(refs[i], held[i], in_sem.at[i]) for i in range(count)]
    stores = [
        pltpu.make_async_copy(held[i], refs[count + i], out_sem.at[i]) for i in range(count)
    ]
    for load in loads:
        load.start()
    for load, store in zip(loads, stores):
        load.wait()
        store.start()
    for store in stores:
        store.wait()


def by_heads(
    queries, key_rows, value_rows, query_tangent, key_tangent, value_tangent, out_weight, upstream
):
    n, ndp = lax.axis_size("seq"), lax.axis_size("dp")
    tok, width = queries.shape[1:]
    model = out_weight.shape[1]
    full = n * tok
    hd = HEAD_DIM
    bf, f32 = jnp.bfloat16, jnp.float32
    rows_dp = width // ndp
    rows_own = rows_dp // n
    any_spec = pl.BlockSpec(memory_space=pltpu.HBM)
    dma = pltpu.SemaphoreType.DMA
    flops = 2 * full * full * hd * 10 + 8 * tok * width * model
    outs = pl.pallas_call(
        functools.partial(fused_kernel, n, ndp),
        out_shape=(
            jax.ShapeDtypeStruct((tok, model), bf),
            jax.ShapeDtypeStruct((tok, model), bf),
            jax.ShapeDtypeStruct((rows_own, model), f32),
            jax.ShapeDtypeStruct((tok, width), bf),
            jax.ShapeDtypeStruct((tok, width), bf),
            jax.ShapeDtypeStruct((tok, width), bf),
        ),
        in_specs=[any_spec] * 8,
        out_specs=(any_spec,) * 6,
        scratch_shapes=[
            pltpu.VMEM((full, 2 * hd), bf),
            pltpu.VMEM((full, 2 * hd), bf),
            pltpu.VMEM((full, 2 * hd), bf),
            pltpu.VMEM((n // 2, full, 2 * tok), bf),
            pltpu.VMEM((full, hd), bf),
            pltpu.VMEM((full, hd), bf),
            pltpu.VMEM((tok, width), bf),
            pltpu.VMEM((tok, width), bf),
            pltpu.VMEM((width, model), bf),
            pltpu.VMEM((tok, model), bf),
            pltpu.VMEM((ndp * tok, model), bf),
            pltpu.VMEM((ndp * tok, rows_dp), bf),
            pltpu.VMEM((tok, width), bf),
            pltpu.VMEM((full, hd), bf),
            pltpu.VMEM((full, hd), f32),
            pltpu.VMEM((full, hd), bf),
            pltpu.VMEM((full, hd), bf),
            pltpu.VMEM((full, hd), bf),
            pltpu.VMEM((2, n // 2, rows_own, model), bf),
            pltpu.VMEM((n // 2, 2, rows_own, model), bf),
            pltpu.VMEM((full, full), f32),
            pltpu.VMEM((full, full), bf),
            pltpu.VMEM((full, full), bf),
            pltpu.VMEM((tok, model), bf),
            pltpu.VMEM((tok, model), bf),
            pltpu.VMEM((rows_own, model), f32),
            pltpu.VMEM((rows_own, model), bf),
            pltpu.VMEM((rows_own, model), bf),
            pltpu.VMEM((full, 1), f32),
            pltpu.VMEM((full, 1), f32),
            pltpu.VMEM((full, hd), f32),
            dma((6, n)), dma((6, n)), dma((2, n)), dma((2, n)), dma((n,)), dma((n,)),
            dma((3, n)), dma((3, n)), dma((n,)), dma((n,)), dma((ndp,)), dma((ndp,)),
            dma((ndp,)), dma((ndp,)), dma((2,)),
            dma((1,)), dma((1,)), dma((3,)),
        ],
        compiler_params=pltpu.CompilerParams(
            collective_id=0, has_side_effects=True, vmem_limit_bytes=60 * 1024 * 1024
        ),
        cost_estimate=pl.CostEstimate(
            flops=flops, bytes_accessed=20 * tok * width, transcendentals=full * full
        ),
    )(
        queries[0], key_rows[0], value_rows[0], query_tangent[0], key_tangent[0],
        value_tangent[0], out_weight, upstream[0],
    )
    block, tan, gw, gq, gk, gv = pl.pallas_call(
        hand_over,
        out_shape=tuple(jax.ShapeDtypeStruct(o.shape, o.dtype) for o in outs),
        in_specs=[any_spec] * 6,
        out_specs=(any_spec,) * 6,
        scratch_shapes=[pltpu.VMEM(o.shape, o.dtype) for o in outs] + [dma((6,)), dma((6,))],
    )(*outs)
    return block[None], tan[None], gw, gq[None], gk[None], gv[None]


def solution(mesh):
    fits = mesh.shape["seq"] == HEADS and mesh.shape["dp"] == 4
    placed = (
        P("dp", "seq", None),
        P("dp", "seq", None),
        P("dp", "seq", None),
        P("dp", "seq", None),
        P("dp", "seq", None),
        P("dp", "seq", None),
        P(),
        P("dp", "seq", None),
    )
    return jax.shard_map(
        by_heads if fits else per_device,
        mesh=mesh,
        in_specs=placed,
        out_specs=(
            P("dp", "seq", None),
            P("dp", "seq", None),
            P(("dp", "seq"), None),
            P("dp", "seq", None),
            P("dp", "seq", None),
            P("dp", "seq", None),
        ),
        check_vma=False,
    )
```
